32 devices in a mesh: obj: 2 (over core), dp: 4 (over y, x), mp: 4 (over z).
Axes of the slice: x: 2, y: 2, z: 4, core: 2. Of those that a mesh axis runs over, the one named last changes fastest.
Arguments:
- layer_input: bfloat16 [8, 768, 2048], P(('obj', 'dp')), may hold values from -6 to 6
- out_grad: bfloat16 [8, 768, 2048], P(('obj', 'dp')), may hold values from -6 to 6
- segment_ids: int32 [8, 768], P(('obj', 'dp')), may hold values from 0 to 2, as said below
- target_flags: int32 [8, 768], P(('obj', 'dp')), may hold values from 0 to 1, as said below
- hidden_units: int32 [4], P('mp'), may hold values from 1 to 2048, as said below
- block_slot: int32 [4, 16], P('mp'), may hold values from 0 to 15, as said below
- weight_blocks: float32 [4, 16, 1024, 1024], P('mp', 'dp'), may hold values from -0.125 to 0.125
- stats_left: float32 [4, 16, 1024, 1024], P('mp', 'dp'), as said below
- stats_right: float32 [4, 16, 1024, 1024], P('mp', 'dp'), as said below
- roots_left: float32 [4, 16, 1024, 1024], P('mp', 'dp'), as said below
- roots_right: float32 [4, 16, 1024, 1024], P('mp', 'dp'), as said below
- norm_params: float32 [4, 2048], replicated
- norm_moments: float32 [4, 2048], replicated, may hold values from 3.8146973e-06 to 1.5258789e-05
Outputs:
- y_out: bfloat16 [8, 768, 2048], P(('obj', 'dp'))
- x_grad: bfloat16 [8, 768, 2048], P(('obj', 'dp'))
- clipped_grads: float32 [4, 16, 1024, 1024], P('mp', 'dp')
- new_weights: float32 [4, 16, 1024, 1024], P('mp', 'dp')
- new_left: float32 [4, 16, 1024, 1024], P('mp', 'dp')
- new_right: float32 [4, 16, 1024, 1024], P('mp', 'dp')
- param_clipped: float32 [4, 2048], replicated
- new_moments: float32 [4, 2048], replicated
- new_params: float32 [4, 2048], replicated
- grad_norm: float32 [], replicated
The draws below stay inside these ranges and needn't reach their ends.
Inputs may be any that keep to these rules, and one draw needn't show every extreme that they name: `segment_ids`: within a row the ids never fall and every row holds all 3 documents; each document holds 1 to 384 positions, one of each row exactly 384. `target_flags`: in the first 4 rows a 1 marks a masked position; in the other rows the ones of a row form one contiguous span of one or more positions. `hidden_units`: they sum to 5461; one index of mp holds exactly 2048. `block_slot`: for each index of mp a permutation of the block numbers; slot s lies on index s // 4 of dp. `stats_left`: Symmetric, with a positive diagonal. `stats_right`: Symmetric, with a positive diagonal. `roots_left`: Symmetric, with a positive diagonal. `roots_right`: Symmetric, with a positive diagonal.
All inputs are finite; a program needn't handle non-finite values.
Results may differ from the reference program's by a relative error of at most 0.0057.
Values may be sent and summed in bfloat16 or wider, within the bound.
No kernel may reach another device: no remote copies, remote signals or barrier semaphores. Data moves between devices by JAX's collectives and lax.ppermute only.
A program may use at most 640 MiB of HBM per device.

```python
import math
import jax
import jax.numpy as jnp
from jax import lax

D = 2048
HEADS = 16
HD = 128
FF = 5461
LEN = 768
SEGS = 3
HCAP = 2048
BLOCK = 1024
ROWS_DEV = 1
ROWS = 8
PANEL = 8192
NBLK = 16
N_MP = 4


def square_blocks(key, scale_value, spread):
    diag_key, noise_key = jax.random.split(key)
    diagonal = scale_value * jnp.exp(jax.random.uniform(diag_key, (N_MP, NBLK, BLOCK), jnp.float32, 0.0, math.log(spread)))
    noise = jax.random.normal(noise_key, (N_MP, NBLK, BLOCK, BLOCK), jnp.float32)
    offdiag = (noise + jnp.swapaxes(noise, 2, 3)) * (0.6 * scale_value / BLOCK ** 0.5)
    identity = jnp.eye(BLOCK, dtype=jnp.float32)
    return offdiag * (1.0 - identity) + diagonal[..., None] * identity


def document_ids(key):
    key = jax.random.fold_in(key, 5)
    long_key, split_key = jax.random.split(key)
    half = LEN // 2
    remain = LEN - half
    least = max(remain // 4, 1)
    long_doc = jax.random.randint(long_key, (ROWS,), 0, SEGS)
    first_other = jax.random.randint(split_key, (ROWS,), least, remain - least + 1)
    doc_index = jnp.arange(SEGS, dtype=jnp.int32)[None, :]
    other_rank = doc_index - (doc_index > long_doc[:, None]).astype(jnp.int32)
    lengths = jnp.where(doc_index == long_doc[:, None], half, jnp.where(other_rank == 0, first_other[:, None], remain - first_other[:, None]))
    ends = jnp.cumsum(lengths, axis=1).astype(jnp.int32)
    position = jnp.arange(LEN, dtype=jnp.int32)[None, :]
    first_mark = (position >= ends[:, 0:1]).astype(jnp.int32)
    second_mark = (position >= ends[:, 1:2]).astype(jnp.int32)
    return (first_mark + second_mark).astype(jnp.int32)


def mix_documents(doc_ids, shared, noise, shared_scale, token_scale):
    doc_part = jax.vmap(lambda table, index: jnp.take(table, index, axis=0))(shared, doc_ids)
    return jnp.clip(shared_scale * doc_part + token_scale * noise, -6.0, 6.0)


def draw_segment_ids(key, part):
    return document_ids(key)


def draw_layer_input(key, part):
    doc_ids = document_ids(key)
    key = jax.random.fold_in(key, 61)
    shared_key, token_key = jax.random.split(key)
    shared = jax.random.normal(shared_key, (ROWS, SEGS, D), jnp.float32)
    noise = jax.random.normal(token_key, (ROWS, LEN, D), jnp.float32)
    return mix_documents(doc_ids, shared, noise, 0.7, 0.7).astype(jnp.bfloat16)


def draw_out_grad(key, part):
    doc_ids = document_ids(key)
    key = jax.random.fold_in(key, 67)
    shared_key, token_key = jax.random.split(key)
    shared = jax.random.normal(shared_key, (ROWS, SEGS, D), jnp.float32)
    noise = jax.random.normal(token_key, (ROWS, LEN, D), jnp.float32)
    return mix_documents(doc_ids, shared, noise, 0.7, 0.7).astype(jnp.bfloat16)


def draw_target_flags(key, part):
    key = jax.random.fold_in(key, 11)
    half_groups = ROWS // (2 * ROWS_DEV)
    denom = max(half_groups - 1, 1)
    row_index = jnp.arange(ROWS, dtype=jnp.int32)
    group_index = row_index // ROWS_DEV % half_groups
    position = jnp.arange(LEN, dtype=jnp.int32)[None, :]
    mask_key, length_key, start_key = jax.random.split(key, 3)
    rate = 60 + 120 * group_index // denom
    picks = jax.random.randint(mask_key, (ROWS, LEN), 0, 1000)
    masked = (picks < rate[:, None]).astype(jnp.int32)
    span_length = LEN * (denom + 2 * group_index) // (10 * denom) + jax.random.randint(length_key, (ROWS,), 0, LEN // 20 + 1)
    span_length = jnp.maximum(span_length, 1)
    span_start = jax.random.randint(start_key, (ROWS,), 0, LEN - span_length + 1)
    inside = (position >= span_start[:, None]) & (position < (span_start + span_length)[:, None])
    return jnp.where((row_index < ROWS // 2)[:, None], masked, inside.astype(jnp.int32)).astype(jnp.int32)


def draw_hidden_units(key, part):
    key = jax.random.fold_in(key, 23)
    others = N_MP - 1
    remain = FF - HCAP
    base_share = remain // others
    extra = remain - base_share * others
    spread = min(HCAP - base_share - 1, base_share) // 2
    full_key, jitter_key = jax.random.split(key)
    jitter = jax.random.randint(jitter_key, (others,), 0, spread + 1)
    order = jnp.arange(others, dtype=jnp.int32)
    shares = base_share + (order < extra).astype(jnp.int32) + jitter - jnp.roll(jitter, 1)
    chosen = jax.random.randint(full_key, (), 0, N_MP)
    ranks = jnp.arange(N_MP, dtype=jnp.int32)
    lookup = jnp.minimum((ranks - chosen - 1) % N_MP, others - 1)
    return jnp.where(ranks == chosen, HCAP, jnp.take(shares, lookup)).astype(jnp.int32)


def draw_block_slot(key, part):
    key = jax.random.fold_in(key, 37)
    rank_keys = jax.random.split(key, N_MP)
    return jax.vmap(lambda single: jax.random.permutation(single, NBLK))(rank_keys).astype(jnp.int32)


def draw_stats_left(key, part):
    key = jax.random.fold_in(key, 41)
    base_scale = BLOCK / (N_MP * D * PANEL)
    return square_blocks(key, base_scale, 4.0)


def draw_stats_right(key, part):
    key = jax.random.fold_in(key, 43)
    base_scale = BLOCK / (N_MP * D * PANEL)
    return square_blocks(key, base_scale, 4.0)


def draw_roots_left(key, part):
    key = jax.random.fold_in(key, 47)
    base_scale = (BLOCK / (N_MP * D * PANEL)) ** (-0.25)
    return square_blocks(key, base_scale, 4.0)


def draw_roots_right(key, part):
    key = jax.random.fold_in(key, 53)
    base_scale = (BLOCK / (N_MP * D * PANEL)) ** (-0.25)
    return square_blocks(key, base_scale, 4.0)


def draw_norm_params(key, part):
    key = jax.random.fold_in(key, 59)
    values = jnp.clip(jax.random.normal(key, (4, D), jnp.float32), -3.0, 3.0)
    parity = (jnp.arange(4, dtype=jnp.int32)[:, None] % 2).astype(jnp.float32)
    return (1.0 - parity) * (1.0 + 0.15 * values) + parity * (0.3 * values)


def block_levels(key, shape, cuts, smallest, top_value):
    level, own = 1.0, jax.random.fold_in(key, 6)
    for dim, parts in cuts:
        steps = jnp.exp(jax.random.uniform(jax.random.fold_in(own, dim), (parts,), jnp.float32, smallest / len(cuts), top_value / len(cuts)))
        level = level * jnp.repeat(steps, shape[dim] // parts).reshape([-1 if axis == dim else 1 for axis in range(len(shape))])
    return level


def gaussian(stream_key, shape, deviation, most, cuts=(), held_as=jnp.bfloat16):
    level = block_levels(stream_key, shape, cuts, -0.22, 0.18) if cuts else 1.0
    entries = jax.random.normal(stream_key, shape, jnp.float32) * deviation * level
    return jnp.minimum(jnp.maximum(entries, -most), most).astype(held_as)


def setup_inputs(seed: int = 0) -> dict:
    splits = jax.random.split(jax.random.key(seed), 14)
    layer_input = draw_layer_input(jax.random.fold_in(splits[13], 71), 0)
    out_grad = draw_out_grad(jax.random.fold_in(splits[13], 71), 0)
    segment_ids = draw_segment_ids(jax.random.fold_in(splits[13], 71), 0)
    target_flags = draw_target_flags(jax.random.fold_in(splits[13], 71), 0)
    hidden_units = draw_hidden_units(jax.random.fold_in(splits[13], 71), 0)
    block_slot = draw_block_slot(jax.random.fold_in(splits[13], 71), 0)
    weight_blocks = gaussian(splits[6], (N_MP, NBLK, BLOCK, BLOCK), D ** -0.5, 0.125, ((0, 4), (1, 4)), jnp.float32)
    stats_left = draw_stats_left(jax.random.fold_in(splits[13], 71), 0)
    stats_right = draw_stats_right(jax.random.fold_in(splits[13], 71), 0)
    roots_left = draw_roots_left(jax.random.fold_in(splits[13], 71), 0)
    roots_right = draw_roots_right(jax.random.fold_in(splits[13], 71), 0)
    norm_params = draw_norm_params(jax.random.fold_in(splits[13], 71), 0)
    norm_moments = jnp.clip(jnp.exp(jax.random.uniform(splits[12], (4, D), jnp.float32, math.log(3.814697265625e-06), math.log(1.52587890625e-05))), 3.814697265625e-06, 1.52587890625e-05)
    return {"layer_input": layer_input, "out_grad": out_grad, "segment_ids": segment_ids, "target_flags": target_flags, "hidden_units": hidden_units, "block_slot": block_slot, "weight_blocks": weight_blocks, "stats_left": stats_left, "stats_right": stats_right, "roots_left": roots_left, "roots_right": roots_right, "norm_params": norm_params, "norm_moments": norm_moments}


@jax.custom_vjp
def low(v):
    return lax.optimization_barrier(v.astype(jnp.bfloat16)).astype(jnp.float32)

@jax.custom_vjp
def low_back(v):
    return v

def low_keep(v):
    return (low(v), None)

def low_pass(kept, grad):
    return (grad,)

def back_keep(v):
    return (v, None)

def back_low(kept, grad):
    return (low(grad),)
low.defvjp(low_keep, low_pass)
low_back.defvjp(back_keep, back_low)
deep_alpha = 48.0 ** 0.5
highest = lax.Precision.HIGHEST

def segment_positions(segment_ids):
    last_axis = segment_ids.ndim - 1
    index = lax.broadcasted_iota(jnp.int32, segment_ids.shape, last_axis)
    earlier = jnp.concatenate([segment_ids[..., :1] - 1, segment_ids[..., :-1]], axis=-1)
    starts = jnp.where(segment_ids != earlier, index, 0).astype(jnp.int32)
    return (index - lax.cummax(starts, axis=last_axis)).astype(jnp.int32)

def rotary_tables(positions, head_dim):
    half_dim = head_dim // 2
    steps_float = jnp.arange(half_dim, dtype=jnp.float32)
    frequency = jnp.exp(-steps_float * (2.0 * math.log(10000.0) / head_dim))
    angle = positions.astype(jnp.float32)[..., None] * frequency
    return (jnp.cos(angle), jnp.sin(angle))

def rotate(value, cosine, sine):
    half_dim = value.shape[-1] // 2
    first_half, second_half = (value[..., :half_dim], value[..., half_dim:])
    cos_wide, sin_wide = (cosine[..., None, :], sine[..., None, :])
    return jnp.concatenate([first_half * cos_wide - second_half * sin_wide, second_half * cos_wide + first_half * sin_wide], axis=-1)

def allowed_mask(segment_ids, spans):
    seq_length = segment_ids.shape[-1]
    index = jnp.arange(seq_length, dtype=jnp.int32)
    causal = index[:, None] >= index[None, :]
    same_doc = segment_ids[..., :, None] == segment_ids[..., None, :]
    visible = (spans[..., None, :] == 0) | (spans[..., :, None] == 1) & causal
    return same_doc & visible

def layer_norm(value, gain, shift):
    center = value - lax.optimization_barrier(jnp.mean(value, axis=-1, keepdims=True))
    inverse = lax.rsqrt(lax.optimization_barrier(jnp.mean(center * center, axis=-1, keepdims=True)) + 1e-05)
    normed = center * inverse
    return normed * gain + shift

def matmul(left, right):
    return jnp.dot(left, right, precision=highest, preferred_element_type=jnp.float32)

def forward_row(panels, norm_params, input_row, segment_row, span_row, position_row, live):
    heads_here = HEADS // N_MP
    local_width = heads_here * HD
    gu_start = 4 * local_width
    cosine, sine = rotary_tables(position_row, HD)
    visible = allowed_mask(segment_row, span_row)
    score_scale = HD ** (-0.5)
    attn_total = jnp.zeros((LEN, D), jnp.float32)
    lowered = []
    for rank in range(N_MP):
        weight_panel = low(panels[rank])
        lowered.append(weight_panel)
        qkv = matmul(input_row, weight_panel[:, :3 * local_width]).reshape(LEN, 3, heads_here, HD)
        query = low(rotate(low_back(qkv[:, 0]), cosine, sine))
        keys_rot = low(rotate(low_back(qkv[:, 1]), cosine, sine))
        values = low(low_back(qkv[:, 2]))
        scores = low_back(jnp.einsum('qhd,khd->hqk', query, keys_rot, precision=highest) * score_scale)
        scores = jnp.where(visible[None], scores, -1000000000.0)
        peak = lax.optimization_barrier(jnp.max(scores, axis=-1, keepdims=True))
        exponent = jnp.exp(scores - peak)
        probs = exponent / lax.optimization_barrier(jnp.sum(exponent, axis=-1, keepdims=True))
        context = jnp.einsum('hqk,khd->qhd', low(probs), values, precision=highest)
        context = low(low_back(context)).reshape(LEN, local_width)
        attn_total = attn_total + matmul(context, weight_panel[:, 3 * local_width:4 * local_width].T)
    attn_out = low_back(attn_total)
    resid_one = deep_alpha * input_row + attn_out
    hidden = layer_norm(resid_one, norm_params[0], norm_params[1])
    hidden_low = low(hidden)
    ffn_total = jnp.zeros((LEN, D), jnp.float32)
    for rank in range(N_MP):
        weight_panel = lowered[rank]
        gate_value = low_back(matmul(hidden_low, weight_panel[:, gu_start:gu_start + HCAP]))
        up_value = low_back(matmul(hidden_low, weight_panel[:, gu_start + HCAP:gu_start + 2 * HCAP]))
        inner = low(jax.nn.gelu(gate_value) * up_value * live[rank])
        ffn_total = ffn_total + matmul(inner, weight_panel[:, gu_start + 2 * HCAP:].T)
    ffn_out = low_back(ffn_total)
    resid_two = deep_alpha * hidden + ffn_out
    return layer_norm(resid_two, norm_params[2], norm_params[3])

def reference(layer_input, out_grad, segment_ids, target_flags, hidden_units, block_slot, weight_blocks, stats_left, stats_right, roots_left, roots_right, norm_params, norm_moments):
    row_blocks = D // BLOCK
    col_blocks = PANEL // BLOCK
    ordered = jax.vmap(lambda blocks, slots: jnp.take(blocks, slots, axis=0))(weight_blocks, block_slot)
    panels = ordered.reshape(N_MP, row_blocks, col_blocks, BLOCK, BLOCK).transpose(0, 1, 3, 2, 4).reshape(N_MP, D, PANEL)
    live = (jnp.arange(HCAP, dtype=jnp.int32)[None, :] < hidden_units[:, None]).astype(jnp.float32)
    flags_float = target_flags.astype(jnp.float32)
    group_total = ROWS // ROWS_DEV
    group_counts = lax.optimization_barrier(jnp.sum(flags_float.reshape(group_total, ROWS_DEV * LEN), axis=1))
    row_weight = jnp.repeat(group_counts * group_total / jnp.sum(group_counts), ROWS_DEV)
    glm_rows = jnp.arange(ROWS, dtype=jnp.int32) >= ROWS // 2
    spans = jnp.where(glm_rows[:, None], target_flags, 0).astype(jnp.int32)
    positions = segment_positions(segment_ids)

    def one_row(carry, items):
        input_row, grad_row, segment_row, span_row, position_row, weight_row = items

        def run(panels_in, params_in, input_in):
            return forward_row(panels_in, params_in, input_in, segment_row, span_row, position_row, live)
        output, pullback = jax.vjp(run, panels, norm_params, input_row)
        panel_grad, param_grad, input_grad = pullback(weight_row * grad_row)
        return ((carry[0] + panel_grad, carry[1] + param_grad), (output.astype(jnp.bfloat16), input_grad.astype(jnp.bfloat16)))
    start = (jnp.zeros((N_MP, D, PANEL), jnp.float32), jnp.zeros((4, D), jnp.float32))
    items = (layer_input.astype(jnp.float32), out_grad.astype(jnp.float32), segment_ids, spans, positions, row_weight)
    (panel_grads, param_grads), (y_out, x_grad) = lax.scan(one_row, start, items)
    block_grads = panel_grads.reshape(N_MP, row_blocks, BLOCK, col_blocks, BLOCK).transpose(0, 1, 3, 2, 4).reshape(N_MP, NBLK, BLOCK, BLOCK)
    slot_grads = jax.vmap(lambda grads, slots: jnp.zeros_like(grads).at[slots].set(grads))(block_grads, block_slot)
    grad_norm = jnp.sqrt(jnp.sum(slot_grads * slot_grads) + jnp.sum(param_grads * param_grads))
    clip_factor = 1.0 / jnp.maximum(grad_norm, 1.0)
    clipped = slot_grads * clip_factor
    new_left = 0.5 * stats_left + 0.5 * jnp.einsum('mbij,mbkj->mbik', clipped, clipped, precision=highest)
    new_right = 0.5 * stats_right + 0.5 * jnp.einsum('mbji,mbjk->mbik', clipped, clipped, precision=highest)
    shaped = jnp.einsum('mbij,mbjk->mbik', jnp.einsum('mbij,mbjk->mbik', roots_left, clipped, precision=highest), roots_right, precision=highest)
    trust = jnp.sqrt(lax.optimization_barrier(jnp.mean(weight_blocks * weight_blocks, axis=(2, 3)))) / jnp.sqrt(lax.optimization_barrier(jnp.mean(shaped * shaped, axis=(2, 3))) + 1e-06)
    new_weights = weight_blocks - 0.3 * trust[..., None, None] * shaped
    param_clipped = param_grads * clip_factor
    new_moments = 0.5 * norm_moments + 0.5 * param_clipped * param_clipped
    new_params = norm_params - 0.1 * param_clipped / (jnp.sqrt(new_moments) + 1e-08)
    return (y_out, x_grad, clipped, new_weights, new_left, new_right, param_clipped, new_moments, new_params, grad_norm)
```

```python
import math

import jax
import jax.numpy as jnp
from jax import lax
from jax.experimental import pallas as pl
from jax.experimental.pallas import tpu as pltpu
from jax.sharding import PartitionSpec as P

HEADS = 16
HD = 128
HCAP = 2048
TILE = 512
PAIR = 2 * HD
CHUNK = 192
STRIP = 16

deep_alpha = 48.0**0.5
stat_decay = 0.5
block_rate = 0.3
param_rate = 0.1
F32 = jnp.float32
BF16 = jnp.bfloat16
VMEM_LIMIT = 60 * 1024 * 1024


def dot(left, right):
    return jnp.dot(left, right, preferred_element_type=F32)


def dot_nt(left, right):
    return lax.dot_general(left, right, (((1,), (1,)), ((), ())), preferred_element_type=F32)


def dot_tn(left, right):
    return lax.dot_general(left, right, (((0,), (0,)), ((), ())), preferred_element_type=F32)


def segment_positions(segment_ids):
    last_axis = segment_ids.ndim - 1
    index = lax.broadcasted_iota(jnp.int32, segment_ids.shape, last_axis)
    earlier = jnp.concatenate([segment_ids[..., :1] - 1, segment_ids[..., :-1]], axis=-1)
    starts = jnp.where(segment_ids != earlier, index, 0)
    return index - lax.cummax(starts, axis=last_axis)


def rotary_tables(positions):
    half_dim = HD // 2
    steps_float = jnp.arange(half_dim, dtype=F32)
    frequency = jnp.exp(-steps_float * (2.0 * math.log(10000.0) / HD))
    angle = positions.astype(F32)[:, None] * frequency
    cosine, sine = jnp.cos(angle), jnp.sin(angle)
    cos_wide = jnp.concatenate([cosine, cosine], axis=1)
    sin_wide = jnp.concatenate([-sine, sine], axis=1)
    return jnp.concatenate([cos_wide, cos_wide], axis=1), jnp.concatenate([sin_wide, sin_wide], axis=1)


def swap_halves(value):
    heads = [
        pltpu.roll(value[:, h * HD : (h + 1) * HD], HD // 2, 1) for h in range(value.shape[1] // HD)
    ]
    return jnp.concatenate(heads, axis=1)


def normalize(value):
    center = value - jnp.mean(value, axis=-1, keepdims=True)
    inverse = lax.rsqrt(jnp.mean(center * center, axis=-1, keepdims=True) + 1e-05)
    return center * inverse, inverse


def norm_backward(grad_out, normed, inverse, gain):
    scaled = grad_out * gain
    first_mean = jnp.mean(scaled, axis=-1, keepdims=True)
    second_mean = jnp.mean(scaled * normed, axis=-1, keepdims=True)
    return inverse * (scaled - first_mean - normed * second_mean)


def add_norm_sums(sums, grad_out, normed):
    rows, width = grad_out.shape
    sums[0:8, :] += jnp.sum((grad_out * normed).reshape(rows // 8, 8, width), axis=0)
    sums[8:16, :] += jnp.sum(grad_out.reshape(rows // 8, 8, width), axis=0)


def each_rows(rows, action):
    def step(i, carry):
        action(pl.ds(pl.multiple_of(i * STRIP, STRIP), STRIP))
        return carry

    lax.fori_loop(0, rows // STRIP, step, 0, unroll=4)


def received(inner, total, sent, rows):
    return jnp.where(inner[0] == 1, total[rows, :], sent[rows, :]).astype(F32)


def axis_sum(value, axes):
    for axis in axes:
        size, step = lax.axis_size(axis), 1
        while step < size:
            value = value + lax.ppermute(value, axis, [(i, i ^ step) for i in range(size)])
            step *= 2
    return value


def after(value, *others):
    return lax.optimization_barrier((value, *others))[0]


PAIRS = [(0, 1), (1, 0), (2, 3), (3, 2)]
MIDDLE = [(1, 2), (2, 1)]
CYCLE = 4


def run_slots(parts, computes, inner, before, behind):
    count = len(parts)
    held, totals = list(parts), [None] * count
    paired = middle = None
    done = [parts[-1]]
    for slot in range(count + CYCLE * len(computes) - 1):
        roles = {}
        for k in range(count):
            stage, phase = divmod(slot - k, CYCLE)
            if 0 <= stage < len(computes):
                roles[phase] = (k, stage)
        paired = None if paired is None else after(paired, *done)
        middle = None if middle is None else after(middle, *done)
        started, outgoing, arrived = [], [], paired
        if 2 in roles:
            k = roles[2][0]
            outgoing.append(held[k] + middle)
        if 0 in roles:
            outgoing.append(held[roles[0][0]])
        sending = None
        if outgoing:
            sending = outgoing[0] if len(outgoing) == 1 else jnp.where(inner, *outgoing)
            if paired is not None and len(outgoing) == 1:
                sending = after(sending, paired)
            started.append(sending)
        crossing = None
        if 1 in roles:
            k = roles[1][0]
            crossing = held[k] = held[k] + paired
            started.append(crossing)
        if 2 in roles:
            totals[roles[2][0]] = sending
        middle = None if crossing is None else lax.ppermute(crossing, "mp", MIDDLE)
        paired = None if sending is None else lax.ppermute(sending, "mp", PAIRS)
        done = []
        if slot in before:
            started.append(before[slot](*started, arrived))
        if 3 in roles:
            k, stage = roles[3]
            held[k] = computes[stage](k, totals[k], after(arrived, *started))
            done.append(held[k])
        if slot in behind:
            done.append(behind[slot](*done, *started))
        if not done:
            done = started
        if slot + 2 < count:
            done = [*done, parts[slot + 2]]


class Panel:
    def __init__(self, blocks, order, row_blocks):
        count, block, _ = blocks.shape
        self.order = order
        self.half = block // 2
        self.pieces = blocks.reshape(2 * count, self.half, block)
        self.col_blocks = count // row_blocks
        self.count = 2 * row_blocks

    def piece(self, order, place, col_block):
        return (place // 2 * self.col_blocks + col_block) * 2 + place % 2

    def specs(self, width, col_block, col_part):
        out = []
        for place in range(self.count):

            def index(step, order, place=place):
                return (self.piece(order, place, col_block(step)), 0, col_part(step))

            out.append(pl.BlockSpec((None, self.half, width), index))
        return out


class HiddenPanel:
    def __init__(self, slices, order, row_blocks):
        self.slices = slices
        self.order = order
        self.ranks = slices.shape[0] // 2
        self.rows, self.block = slices.shape[2:]
        self.half = self.ranks * self.rows
        self.col_blocks = slices.shape[1] // row_blocks
        self.count = 2 * row_blocks

    def copy(self, copies, slices, place, col_block, target):
        source = slices.at[pl.ds(place % 2 * self.ranks, self.ranks), place // 2 * self.col_blocks + col_block]
        return copies.start(source, target.at[pl.ds(place * self.ranks, self.ranks)])

    def held(self, number):
        return pltpu.VMEM((number, self.count * self.ranks, self.rows, self.block), BF16)


def whole(shape):
    zeros = (0,) * len(shape)
    return pl.BlockSpec(shape, lambda step, *_: zeros)


def params():
    return pltpu.CompilerParams(vmem_limit_bytes=VMEM_LIMIT)


def cost(micros):
    return pl.CostEstimate(flops=0, bytes_accessed=int(micros * 3.5e6), transcendentals=0)


def project(rows, pieces):
    half = pieces[0].shape[0]
    total = dot(rows[:, :half], pieces[0][...])
    for k in range(1, len(pieces)):
        total = total + dot(rows[:, k * half : (k + 1) * half], pieces[k][...])
    return total


def qkv_forward(panel, tokens, cosine, sine, local_width):
    length, width = tokens.shape
    count, half, block = panel.count, panel.half, panel.pieces.shape[2]

    def body(order, x, cos, sin, w_qk, w_v, q_out, k_out, v_out, acc):
        step = pl.program_id(0)

        @pl.when(step == 0)
        def _():
            acc[:, : 2 * local_width] = dot(x[...], w_qk[...])
            acc[:, 2 * local_width :] = dot(x[...], w_v[...])

        @pl.when(step > 0)
        def _():
            acc[:, : 2 * local_width] += dot(x[...], w_qk[...])
            acc[:, 2 * local_width :] += dot(x[...], w_v[...])

        @pl.when(step == count - 1)
        def _():
            for i, out in enumerate((q_out, k_out)):
                for h in range(local_width // HD):
                    value = acc[:, i * local_width + h * HD : i * local_width + (h + 1) * HD]
                    turned = pltpu.roll(value, HD // 2, 1)
                    out[:, h * HD : (h + 1) * HD] = (value * cos[:, :HD] + turned * sin[:, :HD]).astype(BF16)
            v_out[...] = acc[:, 2 * local_width :].astype(BF16)

    def weight(col_block, size):
        return pl.BlockSpec(
            (None, half, size), lambda s, order: (panel.piece(order, s, col_block), 0, 0)
        )

    return pl.pallas_call(
        body,
        grid_spec=pltpu.PrefetchScalarGridSpec(
            num_scalar_prefetch=1,
            grid=(count,),
            in_specs=[
                pl.BlockSpec((length, half), lambda s, order: (0, s)),
                whole((length, PAIR)),
                whole((length, PAIR)),
                weight(0, block),
                weight(1, local_width),
            ],
            out_specs=[whole((length, local_width))] * 3,
            scratch_shapes=[pltpu.VMEM((length, 3 * local_width), F32)],
        ),
        out_shape=[jax.ShapeDtypeStruct((length, local_width), BF16)] * 3,
        compiler_params=params(),
        cost_estimate=cost(11),
        name="qkv_forward",
    )(panel.order, tokens, cosine, sine, panel.pieces, panel.pieces)


def attend(panel, chunk, q, k, v, seg_col, seg_row, key_col, col_key):
    length, local_width = q.shape
    pairs = local_width // PAIR
    count, half = panel.count, panel.half
    width = count * half
    scale = HD**-0.5

    def body(order, q_in, k_in, v_in, segc, segr, keyc, colk, *refs):
        wo = refs[:count]
        p_out, c_out, a_out, acc = refs[count:]
        step = pl.program_id(0)

        @pl.when(step == 0)
        def _():
            acc[...] = jnp.zeros_like(acc)

        visible = (segc[...] == segr[...]) & (colk[...] <= keyc[...])
        for h in range(2):
            lanes = slice(h * HD, (h + 1) * HD)
            scores = dot_nt(q_in[:, lanes], k_in[:, lanes]) * scale
            scores = jnp.where(visible, scores, -1000000000.0)
            exponent = jnp.exp(scores - jnp.max(scores, axis=-1, keepdims=True))
            probs = exponent * (1.0 / jnp.sum(exponent, axis=-1, keepdims=True))
            probs = probs.astype(BF16)
            p_out[h] = probs
            c_out[:, lanes] = dot(probs, v_in[:, lanes]).astype(BF16)
        for i in range(count):
            cols = slice(i * half, (i + 1) * half)
            acc[:, cols] += dot_nt(c_out[...], wo[i][...])

        @pl.when(step == pairs - 1)
        def _():
            a_out[...] = acc[...].astype(BF16)

    all_spec = pl.BlockSpec((length, PAIR), lambda s, *_: (0, s))
    column = pl.BlockSpec((CHUNK, 1), lambda s, *_: (chunk, 0))
    return pl.pallas_call(
        body,
        grid_spec=pltpu.PrefetchScalarGridSpec(
            num_scalar_prefetch=1,
            grid=(pairs,),
            in_specs=[
                pl.BlockSpec((CHUNK, PAIR), lambda s, *_: (chunk, s)),
                all_spec,
                all_spec,
                column,
                whole((1, length)),
                column,
                whole((1, length)),
            ]
            + panel.specs(PAIR, lambda s: 1, lambda s: pairs + s),
            out_specs=[
                pl.BlockSpec((2, CHUNK, length), lambda s, *_: (s, 0, 0)),
                pl.BlockSpec((CHUNK, PAIR), lambda s, *_: (0, s)),
                whole((CHUNK, width)),
            ],
            scratch_shapes=[pltpu.VMEM((CHUNK, width), F32)],
        ),
        out_shape=[
            jax.ShapeDtypeStruct((2 * pairs, CHUNK, length), BF16),
            jax.ShapeDtypeStruct((CHUNK, local_width), BF16),
            jax.ShapeDtypeStruct((CHUNK, width), BF16),
        ],
        compiler_params=params(),
        cost_estimate=cost(7),
        name="attend",
    )(panel.order, q, k, v, seg_col, seg_row, key_col, col_key, *[panel.pieces] * count)


def attend_backward(
    panel, chunk, last, inner, state, q, k, v, probs, context, cosine, sine, carried, g1_before
):
    tokens, norm, attn, grad_two, back = state
    length, local_width = q.shape
    width = tokens.shape[1]
    pairs = local_width // PAIR
    count = panel.count
    scale = HD**-0.5
    first = carried is None

    def body(order, flag, x, gains, t1, s1, g2, t3, s3, q_in, k_in, v_in, p_in, c_in, cos, sin, *refs):
        wo = refs[:count]
        refs = refs[count:]
        if not first:
            kg_in, vg_in = refs[:2]
            refs = refs[3:]
        g1_out, low_out, sums, qg_out, kg_out, vg_out, cg, kg = refs
        step = pl.program_id(0)

        @pl.when(step == 0)
        def _():
            sums[...] = jnp.zeros_like(sums)

            def strip(rows):
                resid = deep_alpha * x[rows, :].astype(F32) + received(flag, t1, s1, rows)
                normed, inverse = normalize(resid)
                grad = deep_alpha * g2[rows, :] + received(flag, t3, s3, rows)
                add_norm_sums(sums, grad, normed)
                grad_one = norm_backward(grad, normed, inverse, gains[0:1, :])
                g1_out[rows, :] = grad_one
                low_out[rows, :] = grad_one.astype(BF16)

            each_rows(CHUNK, strip)

        cg[...] = project(low_out[...], wo).astype(BF16)
        for h in range(2):
            lanes = slice(h * HD, (h + 1) * HD)
            cg_rows = cg[:, lanes]
            row_dot = jnp.sum(cg_rows.astype(F32) * c_in[:, lanes].astype(F32), axis=-1, keepdims=True)
            prob_grad = dot_nt(cg_rows, v_in[:, lanes])
            probs_low = p_in[h]
            score_grad = (probs_low.astype(F32) * (prob_grad - row_dot)).astype(BF16)
            raw = dot(score_grad, k_in[:, lanes]) * scale
            own = pl.ds(chunk * CHUNK, CHUNK)
            turned = pltpu.roll(raw, HD // 2, 1)
            qg_out[:, lanes] = (raw * cos[own, lanes] - turned * sin[own, lanes]).astype(BF16)
            key_grad = dot_tn(score_grad, q_in[:, lanes]) * scale
            value_grad = dot_tn(probs_low, cg_rows)
            if not first:
                key_grad = key_grad + kg_in[:, lanes]
                value_grad = value_grad + vg_in[:, lanes]
            vg_out[:, lanes] = value_grad.astype(vg_out.dtype)
            if last:
                kg[:, lanes] = key_grad
            else:
                kg_out[:, lanes] = key_grad
        if last:
            value = kg[...]
            kg_out[...] = (value * cos[...] - swap_halves(value) * sin[...]).astype(BF16)

    head_spec = pl.BlockSpec((length, PAIR), lambda s, *_: (0, s))
    own_head = pl.BlockSpec((CHUNK, PAIR), lambda s, *_: (0, s))
    rows_spec = whole((CHUNK, width))
    kind = BF16 if last else F32
    in_specs = [pl.BlockSpec((CHUNK, width), lambda s, *_: (chunk, 0)), whole((4, width))]
    in_specs += [rows_spec] * 5
    in_specs += [pl.BlockSpec((CHUNK, PAIR), lambda s, *_: (chunk, s)), head_spec, head_spec]
    in_specs += [pl.BlockSpec((2, CHUNK, length), lambda s, *_: (s, 0, 0)), own_head]
    in_specs += [whole((length, PAIR))] * 2
    in_specs += with_scalars(panel.specs(PAIR, lambda s: 1, lambda s: pairs + s))
    operands = [tokens, norm, *attn, grad_two, *back, q, k, v, probs, context, cosine, sine]
    operands += [panel.pieces] * count
    if not first:
        in_specs += [head_spec] * 2 + any_specs(1)
        operands += [*carried, g1_before]
    g1, low_grad, sums, qg, kg, vg = pl.pallas_call(
        body,
        grid_spec=pltpu.PrefetchScalarGridSpec(
            num_scalar_prefetch=2,
            grid=(pairs,),
            in_specs=in_specs,
            out_specs=[
                pl.BlockSpec((CHUNK, width), lambda s, *_: (chunk, 0)),
                rows_spec,
                whole((16, width)),
                own_head,
                head_spec,
                head_spec,
            ],
            scratch_shapes=[pltpu.VMEM((CHUNK, PAIR), BF16), pltpu.VMEM((length, PAIR), F32)],
        ),
        out_shape=[
            jax.ShapeDtypeStruct((length, width), F32),
            jax.ShapeDtypeStruct((CHUNK, width), BF16),
            jax.ShapeDtypeStruct((16, width), F32),
            jax.ShapeDtypeStruct((CHUNK, local_width), BF16),
            jax.ShapeDtypeStruct((length, local_width), kind),
            jax.ShapeDtypeStruct((length, local_width), kind),
        ],
        input_output_aliases={} if first else {1 + len(operands): 0},
        compiler_params=params(),
        cost_estimate=cost(12),
        name="attend_backward",
    )(panel.order, inner, *operands)
    return g1, low_grad, sums, qg, (kg, vg)


def input_parts(panel, q_grad, k_grad, v_grad):
    chunks = len(q_grad)
    length, local_width = k_grad.shape
    count, half = panel.count, panel.half

    def body(order, *refs):
        qg, kg, vg = refs[:chunks], refs[chunks], refs[chunks + 1]
        wq, wk, wv, out = refs[chunks + 2 :]
        out[...] = (
            dot_nt(stack(qg), wq[...]) + dot_nt(kg[...], wk[...]) + dot_nt(vg[...], wv[...])
        ).astype(BF16)

    def weight(col_block, col_part):
        return pl.BlockSpec(
            (None, half, local_width), lambda s, order: (panel.piece(order, s, col_block), 0, col_part)
        )

    return pl.pallas_call(
        body,
        grid_spec=pltpu.PrefetchScalarGridSpec(
            num_scalar_prefetch=1,
            grid=(count,),
            in_specs=[whole((CHUNK, local_width))] * chunks
            + [whole((length, local_width))] * 2
            + [weight(0, 0), weight(0, 1), weight(1, 0)],
            out_specs=pl.BlockSpec((length, half), lambda s, *_: (0, s)),
        ),
        out_shape=jax.ShapeDtypeStruct((length, count * half), BF16),
        compiler_params=params(),
        cost_estimate=cost(10),
        name="input_parts",
    )(panel.order, *q_grad, k_grad, v_grad, *[panel.pieces] * 3)


def span_of(place, size):
    return pl.ds(pl.multiple_of(place * size, size), size)


def with_scalars(specs):
    return [
        pl.BlockSpec(s.block_shape, lambda step, order, *_, f=s.index_map: f(step, order)) for s in specs
    ]


class Copies:
    def __init__(self, sems):
        self.sems = sems
        self.count = 0

    def start(self, source, target):
        copy = pltpu.make_async_copy(source, target, self.sems.at[self.count])
        copy.start()
        self.count += 1
        return copy


def wait_all(copies):
    for copy in copies:
        copy.wait()


def held_rows(held, place, k, cols):
    per = TILE // held.shape[2]
    return held[place, k * per : (k + 1) * per, :, cols].reshape(TILE, cols.stop - cols.start)


def rising(rows, held, place, cols):
    total = None
    for k in range(rows.shape[1] // TILE):
        product = dot(rows[:, k * TILE : (k + 1) * TILE], held_rows(held, place, k, cols))
        total = product if total is None else total + product
    return total


def falling(acc, value, held, place, cols, first):
    for k in range(acc.shape[1] // TILE):
        span = slice(k * TILE, (k + 1) * TILE)
        product = dot_nt(value, held_rows(held, place, k, cols))
        if first:
            acc[:, span] = product
        else:
            acc[:, span] += product


def any_specs(count):
    return [pl.BlockSpec(memory_space=pl.ANY)] * count


def ffn_forward(panel, chunk, scalars, tokens, norm, total, sent, before):
    width = tokens.shape[1]
    block = panel.block
    span = HCAP // block
    own = pl.ds(chunk * CHUNK, CHUNK)

    def body(order, flags, gains, x_in, t_in, s_in, slices, *refs):
        refs = refs[len(before) :]
        hid_out, low_out, act_out, slope_out, inner_out, f_out = refs[:6]
        x, t1, s1, hid, low, act, slope, inner, f, acc, held, sems = refs[6:]
        copies = Copies(sems)
        rows_in = [copies.start(a, b) for a, b in ((t_in, t1), (s_in, s1), (x_in.at[own], x))]
        weights = {
            (tile, group): [
                panel.copy(copies, slices, k, group * span + tile, held.at[tile * 3 + group])
                for k in range(panel.count)
            ]
            for tile in range(span)
            for group in range(3)
        }
        wait_all(rows_in)

        def norm_strip(rows):
            resid = deep_alpha * x[rows, :].astype(F32) + received(flags, t1, s1, rows)
            normed, _ = normalize(resid)
            value = normed * gains[0:1, :] + gains[1:2, :]
            hid[rows, :] = value
            low[rows, :] = value.astype(BF16)

        each_rows(CHUNK, norm_strip)
        out = [copies.start(hid, hid_out), copies.start(low, low_out.at[own])]
        root = math.sqrt(2.0 / math.pi)
        for tile in range(span):
            wait_all(weights[tile, 0])
            wait_all(weights[tile, 1])
            for part in range(block // TILE):
                cols = slice(part * TILE, (part + 1) * TILE)
                gate = rising(low, held, tile * 3, cols)
                up = rising(low, held, tile * 3 + 1, cols)
                lane = lax.broadcasted_iota(jnp.int32, (1, TILE), 1) + (tile * block + part * TILE)
                live = (lane < flags[1]).astype(F32)
                square = gate * gate
                bend = jnp.tanh(root * gate * (1.0 + 0.044715 * square))
                low_half = 0.5 * (1.0 + bend)
                value = gate * low_half * live
                rise = low_half + 0.5 * gate * (1.0 - bend * bend) * (root * (1.0 + 0.134145 * square))
                act[tile, :, cols] = value.astype(BF16)
                slope[tile, :, cols] = (rise * up * live).astype(BF16)
                inner[tile, :, cols] = (value * up).astype(BF16)
                if part == 0:
                    wait_all(weights[tile, 2])
                falling(acc, inner[tile, :, cols], held, tile * 3 + 2, cols, tile == 0 and part == 0)
            cols = pl.ds(tile * block, block)
            for ref, target in ((act, act_out), (slope, slope_out)):
                out.append(copies.start(ref.at[tile], target.at[:, cols]))
            out.append(copies.start(inner.at[tile], inner_out.at[own, cols]))
        f[...] = acc[...].astype(BF16)
        out.append(copies.start(f, f_out))
        wait_all(out)

    tile_shape = jax.ShapeDtypeStruct((CHUNK, HCAP), BF16)
    low_shape = jax.ShapeDtypeStruct((CHUNK, width), BF16)
    low_rows = pltpu.VMEM((CHUNK, width), BF16)
    wide_rows = pltpu.VMEM((CHUNK, width), F32)
    tiles = pltpu.VMEM((span, CHUNK, block), BF16)
    return pl.pallas_call(
        body,
        grid_spec=pltpu.PrefetchScalarGridSpec(
            num_scalar_prefetch=2,
            grid=(1,),
            in_specs=[whole((4, width))] + any_specs(4 + len(before)),
            out_specs=any_specs(6),
            scratch_shapes=[low_rows] * 3
            + [wide_rows, low_rows]
            + [tiles] * 3
            + [low_rows, wide_rows]
            + [
                panel.held(span * 3),
                pltpu.SemaphoreType.DMA((6 + span * (3 * panel.count + 3),)),
            ],
        ),
        out_shape=[
            jax.ShapeDtypeStruct((CHUNK, width), F32),
            jax.ShapeDtypeStruct(tokens.shape, BF16),
            tile_shape,
            tile_shape,
            jax.ShapeDtypeStruct((tokens.shape[0], HCAP), BF16),
            low_shape,
        ],
        input_output_aliases={7: 1, 8: 4} if before else {},
        compiler_params=params(),
        cost_estimate=cost(14),
        name="ffn_forward",
    )(panel.order, scalars, norm, tokens, total, sent, panel.slices, *before)


def ffn_backward(
    panel, chunk, inner, group_weight, hidden, norm, total, sent, out_grad, act, slope, before
):
    width = hidden.shape[1]
    block = panel.block
    span = HCAP // block
    own = pl.ds(chunk * CHUNK, CHUNK)

    def body(order, flags, scale, gains, hid_in, t_in, s_in, og_in, act_in, slope_in, slices, *refs):
        refs = refs[len(before) :]
        y_out, g2_out, low_out, sums, gate_out, up_out, h_out = refs[:7]
        hid, t2, s2, og, act_rows, slope_rows, y, g2, low, gate, up, h, acc, held, sems = refs[7:]
        copies = Copies(sems)
        pairs = ((t_in, t2), (s_in, s2), (hid_in, hid), (og_in.at[own], og))
        rows_in = [copies.start(a, b) for a, b in pairs]
        saved = [copies.start(act_in, act_rows), copies.start(slope_in, slope_rows)]
        weights = {
            (tile, group): [
                panel.copy(copies, slices, k, group * span + tile, held.at[tile * 3 + group])
                for k in range(panel.count)
            ]
            for tile in range(span)
            for group in (2, 0, 1)
        }
        sums[...] = jnp.zeros_like(sums)
        wait_all(rows_in)

        def norm_strip(rows):
            resid = deep_alpha * hid[rows, :] + received(flags, t2, s2, rows)
            normed, inverse = normalize(resid)
            y[rows, :] = (normed * gains[2:3, :] + gains[3:4, :]).astype(BF16)
            grad = scale[0] * og[rows, :].astype(F32)
            add_norm_sums(sums, grad, normed)
            grad_two = norm_backward(grad, normed, inverse, gains[2:3, :])
            g2[rows, :] = grad_two
            low[rows, :] = grad_two.astype(BF16)

        each_rows(CHUNK, norm_strip)
        out = [copies.start(a, b) for a, b in ((y, y_out.at[own]), (g2, g2_out), (low, low_out.at[own]))]
        wait_all(saved)
        for tile in range(span):
            wait_all(weights[tile, 2])
            for part in range(block // TILE):
                cols = slice(part * TILE, (part + 1) * TILE)
                saved_cols = slice(tile * block + part * TILE, tile * block + (part + 1) * TILE)
                inner_grad = rising(low, held, tile * 3 + 2, cols)
                gate_grad = (inner_grad * slope_rows[:, saved_cols].astype(F32)).astype(BF16)
                up_grad = (inner_grad * act_rows[:, saved_cols].astype(F32)).astype(BF16)
                gate[tile, :, cols] = gate_grad
                up[tile, :, cols] = up_grad
                if part == 0:
                    wait_all(weights[tile, 0])
                    wait_all(weights[tile, 1])
                falling(acc, gate_grad, held, tile * 3, cols, tile == 0 and part == 0)
                falling(acc, up_grad, held, tile * 3 + 1, cols, False)
            cols = pl.ds(tile * block, block)
            for ref, target in ((gate, gate_out), (up, up_out)):
                out.append(copies.start(ref.at[tile], target.at[own, cols]))
        h[...] = acc[...].astype(BF16)
        out.append(copies.start(h, h_out))
        wait_all(out)

    operands = [norm, hidden, total, sent, out_grad, act, slope, panel.slices]
    operands += before
    wide_tile_shape = jax.ShapeDtypeStruct((out_grad.shape[0], HCAP), BF16)
    low_shape = jax.ShapeDtypeStruct((CHUNK, width), BF16)
    low_rows = pltpu.VMEM((CHUNK, width), BF16)
    wide_rows = pltpu.VMEM((CHUNK, width), F32)
    tiles = pltpu.VMEM((span, CHUNK, block), BF16)
    return pl.pallas_call(
        body,
        grid_spec=pltpu.PrefetchScalarGridSpec(
            num_scalar_prefetch=3,
            grid=(1,),
            in_specs=[whole((4, width))] + any_specs(len(operands) - 1),
            out_specs=any_specs(3) + [whole((16, width))] + any_specs(3),
            scratch_shapes=[wide_rows, low_rows, low_rows, low_rows]
            + [pltpu.VMEM((CHUNK, HCAP), BF16)] * 2
            + [low_rows, wide_rows, low_rows, tiles, tiles, low_rows, wide_rows]
            + [
                panel.held(span * 3),
                pltpu.SemaphoreType.DMA((10 + span * (3 * panel.count + 2),)),
            ],
        ),
        out_shape=[
            jax.ShapeDtypeStruct(out_grad.shape, BF16),
            jax.ShapeDtypeStruct((CHUNK, width), F32),
            jax.ShapeDtypeStruct(out_grad.shape, BF16),
            jax.ShapeDtypeStruct((16, width), F32),
            wide_tile_shape,
            wide_tile_shape,
            low_shape,
        ],
        input_output_aliases={11 + i: out for i, out in enumerate((0, 2, 4, 5)[: len(before)])},
        compiler_params=params(),
        cost_estimate=cost(20),
        name="ffn_backward",
    )(panel.order, inner, group_weight, *operands)


def stack(refs):
    return jnp.concatenate([r[...] for r in refs], axis=0)


def turn(left, refs):
    left[...] = stack(refs).T


def grad_outputs(block, blocks, ranks, full=False):
    half = block // 2
    if full:
        return (
            pl.BlockSpec((2 * ranks, None, half // ranks, block), lambda s, *_: (0, s, 0, 0)),
            jax.ShapeDtypeStruct((2 * ranks, blocks, half // ranks, block), BF16),
        )
    if ranks is None:
        return (
            pl.BlockSpec((None, half, block), lambda s, *_: (s, 0, 0)),
            jax.ShapeDtypeStruct((blocks, half, block), BF16),
        )
    return (
        pl.BlockSpec((ranks, None, half // ranks, block), lambda s, *_: (0, s, 0, 0)),
        jax.ShapeDtypeStruct((ranks, blocks, half // ranks, block), BF16),
    )


def ffn_weight_grads(which, left, rights, ranks=None, arrived=None, full=False):
    length, width = left.shape
    block = width // 2
    half = block // 2
    span = HCAP // block
    per_row = len(rights) * span

    rows = block if full else half

    def body(core, g, *refs):
        out, turned = refs[-2:]
        step = pl.program_id(0) % per_row

        @pl.when(step == 0)
        def _():
            turned[...] = g[...].T

        def write(right):
            result = dot(turned[...], right[...])
            if arrived is not None:
                result = result + refs[len(rights)][...].astype(F32)
            out[...] = result.astype(BF16).reshape(out.shape)

        for i, right in enumerate(refs[: len(rights)]):
            pl.when(step // span == i)(lambda right=right: write(right))

    def right_spec(group):
        return pl.BlockSpec(
            (length, block), lambda s, core: (0, jnp.clip(s % per_row - group * span, 0, span - 1))
        )

    if full:
        left_spec = pl.BlockSpec((length, rows), lambda s, core: (0, s // per_row))
    else:
        left_spec = pl.BlockSpec((length, rows), lambda s, core: (0, s // per_row * 2 + core[0]))
    in_specs = [left_spec] + [right_spec(i) for i in range(len(rights))]
    operands = [left, *rights]
    blocks = width // block * per_row
    if arrived is not None:
        in_specs.append(pl.BlockSpec((None, half, block), lambda s, core: (s, 0, 0)))
        operands.append(arrived)
    out_spec, out_shape = grad_outputs(block, blocks, ranks, full)
    return pl.pallas_call(
        body,
        grid_spec=pltpu.PrefetchScalarGridSpec(
            num_scalar_prefetch=1,
            grid=(blocks,),
            in_specs=in_specs,
            out_specs=out_spec,
            scratch_shapes=[pltpu.VMEM((rows, length), BF16)],
        ),
        out_shape=out_shape,
        compiler_params=params(),
        cost_estimate=cost(15),
        name="ffn_weight_grads",
    )(which, *operands)


def halving_bits(ranks, row_block):
    bits = [1 << i for i in range(ranks.bit_length() - 1)]
    return bits if row_block % 2 == 0 else bits[::-1]


def halving_keys(ranks, row_block):
    bits = halving_bits(ranks, row_block)
    return [
        sum(bit for j, bit in enumerate(bits) if i >> (len(bits) - 1 - j) & 1) for i in range(ranks)
    ]


def attention_weight_grads(which, tokens, q_grad, k_grad, v_grad, attn_grad, context, ranks=None, arrived=None):
    length, width = tokens.shape
    chunks = len(context)
    local_width = k_grad.shape[1]
    block = 2 * local_width
    half = block // 2
    row_blocks = width // block
    outputs = 1 if ranks is None else 2 * row_blocks
    rows = half // (ranks or 1)

    def body(core, x, kg, vg, *refs):
        qg, ctx, g = (refs[i * chunks : (i + 1) * chunks] for i in range(3))
        refs = refs[3 * chunks :]
        outs, turned, held = refs[-2 - outputs : -2], refs[-2], refs[-1]
        row_block, step = pl.program_id(0) // 2, pl.program_id(0) % 2

        def write(start, right):
            cols = slice(start, start + local_width)
            result = dot(turned[...], right)
            if arrived is not None:
                result = result + refs[0][:, cols].astype(F32)
            result = result.astype(BF16)
            if ranks is None:
                outs[0][:, cols] = result
                return
            held[...] = result
            for r in range(row_blocks):

                @pl.when(row_block == r)
                def _(r=r):
                    for i, key in enumerate(halving_keys(ranks, r)):
                        own = span_of(core[1] ^ key, rows)
                        outs[2 * r + i // (ranks // 2)][i % (ranks // 2), :, cols] = held[own, :]

        @pl.when(step == 0)
        def _():
            turned[...] = x[...].T
            write(0, stack(qg))
            write(local_width, kg[...])

        @pl.when(step == 1)
        def _():
            write(0, vg[...])
            turn(turned, g)
            write(local_width, stack(ctx))

    in_specs = [pl.BlockSpec((length, half), lambda s, core: (0, s // 2 * 2 + core[0]))]
    in_specs += [whole((length, local_width))] * 2
    in_specs += [whole((CHUNK, local_width))] * (2 * chunks)
    in_specs += [pl.BlockSpec((CHUNK, half), lambda s, core: (0, s // 2 * 2 + core[0]))] * chunks
    operands = [tokens, k_grad, v_grad, *q_grad, *context, *attn_grad]
    if arrived is not None:
        in_specs.append(pl.BlockSpec((None, half, block), lambda s, core: (s, 0, 0)))
        operands.append(arrived)
    if ranks is None:
        out_specs = [pl.BlockSpec((None, half, block), lambda s, *_: (s, 0, 0))]
        out_shape = [jax.ShapeDtypeStruct((2 * row_blocks, half, block), BF16)]
    else:
        out_specs = [
            pl.BlockSpec(
                (ranks // 2, None, rows, block), lambda s, *_, r=i // 2: (0, jnp.clip(s - 2 * r, 0, 1), 0, 0)
            )
            for i in range(outputs)
        ]
        out_shape = [jax.ShapeDtypeStruct((ranks // 2, 2, rows, block), BF16)] * outputs
    return pl.pallas_call(
        body,
        grid_spec=pltpu.PrefetchScalarGridSpec(
            num_scalar_prefetch=1,
            grid=(2 * row_blocks,),
            in_specs=in_specs,
            out_specs=out_specs,
            scratch_shapes=[pltpu.VMEM((half, length), BF16), pltpu.VMEM((half, local_width), BF16)],
        ),
        out_shape=out_shape,
        compiler_params=params(),
        cost_estimate=cost(9),
        name="attention_weight_grads",
    )(which, *operands)


SWAP = [(0, 1), (1, 0)]


class Group:
    def __init__(self, grads):
        self.grads = grads
        self.core = lax.axis_index("obj").astype(jnp.int32).reshape(1)

    def make_away(self, *others):
        self.away = self.grads(after(1 - self.core, *others), None, None)
        return self.away

    def send(self, *others):
        self.arrived = lax.ppermute(after(self.away, *others), "obj", SWAP)
        return self.away

    def reduce(self, earlier, *others):
        own = self.grads(self.core, lax.axis_size("dp"), after(self.arrived, *others))
        operand = after(own, *[group.sum for group in earlier])
        self.sum = lax.psum_scatter(operand, "dp", scatter_dimension=0, tiled=True)[0]
        return own

    def reduce_whole(self, *others):
        own = self.grads(after(self.core, *others), lax.axis_size("dp"), None, True)
        self.sum = lax.psum_scatter(own, ("obj", "dp"), scatter_dimension=0, tiled=True)[0]
        return own


def pick_slices(places, groups, sizes):
    rows, block = groups[0].shape[1:]
    ends, total = [], 0
    for group in groups:
        total += group.shape[0]
        ends.append(total)
    targets = [(array, place) for array, size in enumerate(sizes) for place in range(size)]

    def body(place, *refs):
        sources, outs = refs[: len(groups)], refs[len(groups) : -3]
        held, into, out_of = refs[-3:]
        for i in range(len(targets)):
            for g, source in enumerate(sources):
                first = ends[g - 1] if g else 0

                @pl.when((place[i] >= first) & (place[i] < ends[g]))
                def _(source=source, first=first, i=i):
                    pltpu.make_async_copy(source.at[place[i] - first], held.at[i], into.at[i]).start()

        copies = []
        for i, (array, spot) in enumerate(targets):
            pltpu.make_async_copy(sources[0].at[0], held.at[i], into.at[i]).wait()
            copy = pltpu.make_async_copy(held.at[i], outs[array].at[spot], out_of.at[i])
            copy.start()
            copies.append(copy)
        wait_all(copies)

    return pl.pallas_call(
        body,
        grid_spec=pltpu.PrefetchScalarGridSpec(
            num_scalar_prefetch=1,
            grid=(1,),
            in_specs=any_specs(len(groups)),
            out_specs=any_specs(len(sizes)),
            scratch_shapes=[pltpu.VMEM((len(targets), rows, block), BF16)]
            + [pltpu.SemaphoreType.DMA((len(targets),))] * 2,
        ),
        out_shape=[jax.ShapeDtypeStruct((size, rows, block), BF16) for size in sizes],
        compiler_params=params(),
        cost_estimate=cost(5),
        name="pick_slices",
    )(places, *groups)


def place_blocks(starts, sources):
    slices, count, rows, block = sources[0].shape
    total = len(sources) * slices

    def body(begin, *refs):
        parts, out, held, into, out_of = refs[:-4], *refs[-4:]
        arriving, leaving = [], []
        for i in range(total):
            copy = pltpu.make_async_copy(parts[i // slices].at[i % slices], held.at[i], into.at[i])
            copy.start()
            arriving.append(copy)
        for i in range(total):
            arriving[i].wait()
            own = pl.ds(pl.multiple_of(begin[i], rows), rows)
            for j in range(count):
                target = out.at[i // slices // 2 * count + j, own]
                copy = pltpu.make_async_copy(held.at[i, j], target, out_of.at[i * count + j])
                copy.start()
                leaving.append(copy)
        wait_all(leaving)

    return pl.pallas_call(
        body,
        grid_spec=pltpu.PrefetchScalarGridSpec(
            num_scalar_prefetch=1,
            grid=(1,),
            in_specs=any_specs(len(sources)),
            out_specs=pl.BlockSpec(memory_space=pl.ANY),
            scratch_shapes=[
                pltpu.VMEM((total, count, rows, block), BF16),
                pltpu.SemaphoreType.DMA((total,)),
                pltpu.SemaphoreType.DMA((total * count,)),
            ],
        ),
        out_shape=jax.ShapeDtypeStruct((len(sources) // 2 * count, block, block), BF16),
        compiler_params=params(),
        cost_estimate=cost(6),
        name="place_blocks",
    )(starts, *sources)


def gather_block(starts, slices, grad):
    for i, piece in enumerate(slices):
        rows = piece.shape[0]
        grad[pl.ds(pl.multiple_of(starts[i], rows), rows), :] = piece[...]


def update_blocks(first, starts, scales, slices, roots_left, roots_right, weights, stats_left, stats_right, before):
    count, piece_rows, block = slices[0].shape
    half = block // 2
    steps = 4

    def body(begin, factor, *refs):
        pieces, refs = refs[: len(slices)], refs[len(slices) :]
        left, right, w, sl, sr = refs[:5]
        c_out, w_out, l_out, r_out, grad, inner, shaped, trust = refs[5 + len(before) :]
        slot, part = pl.program_id(0) + first, pl.program_id(1)
        clip = factor[0, slot]

        @pl.when(part == 0)
        def _():
            gather_block(begin, pieces, grad)
            low = (grad[...].astype(F32) * clip).astype(BF16)
            inner[...] = dot(left[...], low).astype(BF16)

        @pl.when(part == 1)
        def _():
            value = dot(inner[...], right[...])
            shaped[...] = value
            energy = jnp.sum(value * value) * (1.0 / (block * block))
            trust[...] = factor[2, slot] / jnp.sqrt(jnp.full((8, 128), energy, F32) + 1e-06)

        @pl.when(part >= 2)
        def _():
            rows = pl.ds(pl.multiple_of((part - 2) * half, half), half)
            w_out[...] = w[...] - trust[0:1, 0:1] * shaped[rows, :]
            own = grad[rows, :]
            c_out[...] = own.astype(F32) * clip
            square = factor[1, slot]
            l_out[...] = stat_decay * sl[...] + square * dot_nt(own, grad[...])
            r_out[...] = stat_decay * sr[...] + square * dot_tn(grad[:, rows], grad[...])

    def ahead(from_step):
        return lambda s, p, *_: jnp.minimum(s + (p >= from_step).astype(jnp.int32), count - 1)

    def full(place):
        return pl.BlockSpec((None, block, block), lambda s, p, *_: (first + place(s, p), 0, 0))

    piece = pl.BlockSpec((None, piece_rows, block), lambda s, p, *_: (ahead(3)(s, p), 0, 0))
    right_place = lambda s, p: jnp.maximum(s - (p < 1).astype(jnp.int32), 0)
    half_spec = pl.BlockSpec((None, half, block), lambda s, p, *_: (first + s, jnp.maximum(p - 2, 0), 0))
    out = jax.ShapeDtypeStruct(weights.shape, F32)
    in_specs = [piece] * len(slices) + [full(ahead(3)), full(right_place)] + [half_spec] * 3
    return pl.pallas_call(
        body,
        grid_spec=pltpu.PrefetchScalarGridSpec(
            num_scalar_prefetch=2,
            grid=(count, steps),
            in_specs=in_specs + any_specs(len(before)),
            out_specs=[half_spec] * 4,
            scratch_shapes=[
                pltpu.VMEM((block, block), BF16),
                pltpu.VMEM((block, block), BF16),
                pltpu.VMEM((block, block), F32),
                pltpu.VMEM((8, 128), F32),
            ],
        ),
        out_shape=[out] * 4,
        input_output_aliases={2 + len(in_specs) + i: i for i in range(len(before))},
        compiler_params=params(),
        cost_estimate=cost(14 * count),
        name="update_blocks",
    )(starts, scales, *slices, roots_left, roots_right, weights, stats_left, stats_right, *before)


def norm_sums(sums):
    return jnp.sum(sum(sums).reshape(2, 8, -1), axis=1)


def per_device(
    layer_input,
    out_grad,
    segment_ids,
    target_flags,
    hidden_units,
    block_slot,
    weight_blocks,
    stats_left,
    stats_right,
    roots_left,
    roots_right,
    norm_params,
    norm_moments,
):
    row_count, length, width = layer_input.shape
    local_width = HEADS // lax.axis_size("mp") * HD
    owned_slots, block = weight_blocks.shape[1], weight_blocks.shape[-1]
    half = block // 2
    slots = block_slot.shape[1]
    core = lax.axis_index("obj")

    master = weight_blocks[0]
    ranks, rank = lax.axis_size("dp"), lax.axis_index("dp").astype(jnp.int32)
    rows, row_blocks = half // ranks, width // block
    core_row = core.astype(jnp.int32) * half
    received_slices = [None] * ranks
    for k in [*range(1, ranks), 0]:
        first_row = core_row + (rank ^ k) * rows
        piece = lax.dynamic_slice(master, (0, first_row, 0), (owned_slots, rows, block)).astype(BF16)
        received_slices[k] = lax.ppermute(piece, "dp", [(i, i ^ k) for i in range(ranks)]) if k else piece
    by_place = block_slot[0].reshape(row_blocks, -1)
    attention_blocks = 4 * local_width // block
    panel_slots = jnp.concatenate([by_place[:, :attention_blocks].reshape(-1), by_place[:, attention_blocks:].reshape(-1)])
    weight_energy = jnp.mean(master * master, axis=(1, 2))
    low_left, low_right = roots_left[0].astype(BF16), roots_right[0].astype(BF16)
    sources = ((panel_slots // owned_slots) ^ rank) * owned_slots + panel_slots % owned_slots
    sources, weight_energy, low_left, low_right = lax.optimization_barrier(
        (sources, weight_energy, low_left, low_right)
    )
    sizes = [attention_blocks] * row_blocks + [slots - attention_blocks * row_blocks]
    *attention_slices, hidden_slices = pick_slices(sources, received_slices, sizes)
    hidden_panel = HiddenPanel(
        lax.all_gather(hidden_slices, ("obj", "dp"), axis=0), block_slot[0], row_blocks
    )
    parts_held, part_starts = [], []
    for row_block, held in enumerate(attention_slices):
        held, keys = held[None], [0]
        bits = [1 << i for i in range(ranks.bit_length() - 1)]
        for bit in bits if row_block % 2 == 0 else bits[::-1]:
            arriving = lax.ppermute(held, "dp", [(i, i ^ bit) for i in range(ranks)])
            held = jnp.concatenate([held, arriving])
            keys = keys + [key ^ bit for key in keys]
        parts_held += [held, lax.ppermute(held, "obj", SWAP)]
        first_rows = (rank ^ jnp.array(keys, jnp.int32)) * rows
        part_starts += [core_row + first_rows, half - core_row + first_rows]
    panel = Panel(place_blocks(jnp.concatenate(part_starts), parts_held), block_slot[0], row_blocks)

    flags = target_flags.reshape(length)
    own_count = jnp.sum(flags.astype(F32))
    total_count = axis_sum(own_count, ("obj", "dp"))
    group_total = lax.axis_size("obj") * lax.axis_size("dp")
    group_weight = own_count * group_total / total_count

    segments = segment_ids.reshape(length)
    cosine, sine = rotary_tables(segment_positions(segment_ids)[0])
    cosine, group_weight = lax.optimization_barrier((cosine, group_weight))
    index = jnp.arange(length, dtype=jnp.int32)
    in_span = (flags == 1) & (core == 1)
    key_col = jnp.where(in_span, index, -1)[:, None]
    col_key = jnp.where(in_span, index, -1)[None, :]

    tokens = layer_input.reshape(length, width)
    chunks = range(length // CHUNK)
    parts = [slice(c * CHUNK, (c + 1) * CHUNK) for c in chunks]
    query, keys_rot, values = qkv_forward(panel, tokens, cosine, sine, local_width)
    masks = (segments[:, None], segments[None, :], key_col, col_key)
    attended = [attend(panel, c, query, keys_rot, values, *masks) for c in chunks]
    probs, context, attn_part = zip(*attended)
    place = lax.axis_index("mp")
    inner_flag = ((place == 1) | (place == 2)).astype(jnp.int32).reshape(1)
    scalars = jnp.concatenate([inner_flag, hidden_units])
    weight_scalar = group_weight.reshape(1)
    flat_out_grad = out_grad.reshape(length, width)
    attn, ahead, back, turned = {}, {}, {}, {}

    def ffn_ahead(c, total, sent):
        attn[c] = (total, sent)
        before = [ahead[c - 1][i] for i in (1, 4)] if c else []
        ahead[c] = ffn_forward(hidden_panel, c, scalars, tokens, norm_params, total, sent, before)
        return ahead[c][5]

    def ffn_back(c, total, sent):
        hidden, _, act, slope, _, _ = ahead[c]
        saved = (hidden, norm_params, total, sent, flat_out_grad, act, slope)
        before = [back[c - 1][i] for i in (0, 2, 4, 5)] if c else []
        back[c] = ffn_backward(hidden_panel, c, inner_flag, weight_scalar, *saved, before)
        return back[c][6]

    def attention_back(c, total, sent):
        if c == len(chunks) - 1:
            total = after(total, down.sum)
        state = (tokens, norm_params, attn[c], back[c][1], (total, sent))
        heads = (query, keys_rot, values, probs[c], context[c], cosine, sine)
        carried = turned[c - 1][4] if c else None
        g1_before = turned[c - 1][0] if c else None
        last = c == len(chunks) - 1
        turned[c] = attend_backward(panel, c, last, inner_flag, state, *heads, carried, g1_before)
        return turned[c][2]

    def each_of(results, i):
        return [results[c][i] for c in chunks]

    last_chunk = chunks[-1]

    def down_grads(which, *opts):
        return ffn_weight_grads(which, back[last_chunk][2], [ahead[last_chunk][4]], *opts)

    def gate_up_grads(which, *opts):
        return ffn_weight_grads(which, ahead[last_chunk][1], list(back[last_chunk][4:6]), *opts)

    def attention_grads(which, *opts):
        heads = (each_of(turned, 3), *turned[chunks[-1]][4], each_of(turned, 1), context)
        return attention_weight_grads(which, tokens, *heads, *opts)

    down, gate_up = Group(down_grads), Group(gate_up_grads)

    first = len(chunks) - 1 + 2 * CYCLE
    before = {
        first: down.reduce_whole,
        first + 1: gate_up.send,
        first + 2: lambda *others: gate_up.reduce((), *others),
    }
    behind = {first: gate_up.make_away}
    run_slots(attn_part, (ffn_ahead, ffn_back, attention_back), inner_flag[0] == 1, before, behind)
    y_out = back[chunks[-1]][0].reshape(row_count, length, width)
    sums_two = each_of(back, 3)
    sums_one, query_grad = each_of(turned, 2), each_of(turned, 3)
    def squares(value):
        wide = value.astype(F32)
        return jnp.sum(wide * wide)

    own_core = core.astype(jnp.int32)
    (away,) = attention_grads(jnp.stack([1 - own_core, rank]))
    arrived = lax.ppermute(away, "obj", SWAP)
    input_part = input_parts(panel, [after(query_grad[0], away)] + query_grad[1:], *turned[chunks[-1]][4])
    own_norm_grad = jnp.concatenate([norm_sums(sums_one), norm_sums(sums_two)])
    norm_grad = axis_sum(after(own_norm_grad, away), ("obj", "dp"))
    halved = attention_grads(jnp.stack([own_core, rank]), ranks, after(arrived, input_part, norm_grad))
    early_squares = squares(gate_up.sum) + squares(down.sum)
    attention_sums = []
    for row_block in range(row_blocks):
        kept, sent = halved[2 * row_block : 2 * row_block + 2]
        for bit in halving_bits(ranks, row_block):
            arriving = lax.ppermute(sent, "dp", [(i, i ^ bit) for i in range(ranks)])
            if kept.shape[0] == 1:
                arriving = after(arriving, early_squares)
            total = kept + arriving
            kept, sent = total[: total.shape[0] // 2], total[total.shape[0] // 2 :]
        attention_sums.append(total[0])
    input_sum = lax.psum(after(input_part, gate_up.sum), "mp")

    groups = (*attention_sums, gate_up.sum, down.sum)
    own_squares = axis_sum(early_squares + sum(squares(group) for group in attention_sums), ("mp",))
    others = rank ^ jnp.arange(ranks, dtype=jnp.int32)
    col_blocks = slots // (width // block)
    place_of, firsts, base = [0] * slots, (0, 2, 2 + 2 * (HCAP // block), col_blocks), 0
    for first, stop in zip(firsts, firsts[1:]):
        for row_block in range(width // block):
            for col_block in range(first, stop):
                place_of[row_block * col_blocks + col_block] = base
                base += 1
    slot_index = jnp.arange(slots, dtype=jnp.int32)
    at_slot = jnp.sum(
        jnp.where(block_slot[0][None, :] == slot_index[:, None], jnp.array(place_of, jnp.int32)[None, :], 0),
        axis=1,
    )
    wanted = jnp.take(at_slot.reshape(ranks, owned_slots), others, axis=0).reshape(-1)
    halves = 2 if owned_slots % 2 == 0 else 1
    each = owned_slots // halves
    wanted = wanted.reshape(ranks, halves, each).transpose(1, 0, 2).reshape(-1)
    picked = pick_slices(wanted, groups, [each] * (halves * ranks))
    first_rows = others * rows
    starts = jnp.concatenate([core_row + first_rows, half - core_row + first_rows])
    low_roots = (low_left, low_right)

    def exchange(part, *earlier):
        pieces = [after(piece, *earlier) for piece in picked[part * ranks : (part + 1) * ranks]]
        mine = [
            lax.ppermute(piece, "dp", [(i, i ^ k) for i in range(ranks)]) if k else piece
            for k, piece in enumerate(pieces)
        ]
        return mine

    def hand_over(mine):
        return mine + [lax.ppermute(piece, "obj", SWAP) for piece in mine]

    rank_squares = [own_squares] + [
        lax.ppermute(own_squares, "dp", [(i, i ^ k) for i in range(ranks)]) for k in range(1, ranks)
    ]
    core_squares = jnp.sum(jnp.stack(rank_squares)[others])
    block_squares = axis_sum(core_squares, ("obj",))
    grad_norm = jnp.sqrt(block_squares + jnp.sum(norm_grad * norm_grad))
    clip_factor = 1.0 / jnp.maximum(grad_norm, 1.0)

    exchanged = [exchange(0, *rank_squares)]
    if halves == 2:
        exchanged.append(exchange(1, *exchanged[0], clip_factor))
    clips = jnp.full((owned_slots,), clip_factor, F32)
    scales = jnp.stack([clips, (1.0 - stat_decay) * clips * clips, block_rate * jnp.sqrt(weight_energy)])
    results = ()
    for part in range(halves):
        slices = hand_over([after(piece, *results[:1]) for piece in exchanged[part]])
        results = update_blocks(
            part * each, starts, scales, slices, *low_roots, master, stats_left[0], stats_right[0], results
        )
    clipped, new_weights, new_left, new_right = results
    x_grad = (deep_alpha * turned[chunks[-1]][0] + input_sum.astype(F32)).astype(BF16)
    x_grad = x_grad.reshape(row_count, length, width)
    param_clipped = norm_grad * clip_factor
    new_moments = 0.5 * norm_moments + 0.5 * param_clipped * param_clipped
    new_params = norm_params - param_rate * param_clipped / (jnp.sqrt(new_moments) + 1e-08)
    return (
        y_out,
        x_grad,
        clipped[None],
        new_weights[None],
        new_left[None],
        new_right[None],
        param_clipped,
        new_moments,
        new_params,
        grad_norm,
    )


def solution(mesh):
    return jax.shard_map(
        per_device,
        mesh=mesh,
        in_specs=(
            P(("obj", "dp"), None, None),
            P(("obj", "dp"), None, None),
            P(("obj", "dp"), None),
            P(("obj", "dp"), None),
            P("mp"),
            P("mp", None),
            P("mp", "dp", None, None),
            P("mp", "dp", None, None),
            P("mp", "dp", None, None),
            P("mp", "dp", None, None),
            P("mp", "dp", None, None),
            P(),
            P(),
        ),
        out_specs=(
            P(("obj", "dp"), None, None),
            P(("obj", "dp"), None, None),
            P("mp", "dp", None, None),
            P("mp", "dp", None, None),
            P("mp", "dp", None, None),
            P("mp", "dp", None, None),
            P(),
            P(),
            P(),
            P(),
        ),
        check_vma=False,
    )
```

```python
import math

import jax
import jax.numpy as jnp
from jax import lax
from jax.experimental import pallas as pl
from jax.experimental.pallas import tpu as pltpu
from jax.sharding import PartitionSpec as P

HEADS = 16
HD = 128
HCAP = 2048
TILE = 512
PAIR = 2 * HD
CHUNK = 192
STRIP = 16

deep_alpha = 48.0**0.5
stat_decay = 0.5
block_rate = 0.3
param_rate = 0.1
F32 = jnp.float32
BF16 = jnp.bfloat16
VMEM_LIMIT = 60 * 1024 * 1024


def dot(left, right):
    return jnp.dot(left, right, preferred_element_type=F32)


def dot_nt(left, right):
    return lax.dot_general(left, right, (((1,), (1,)), ((), ())), preferred_element_type=F32)


def dot_tn(left, right):
    return lax.dot_general(left, right, (((0,), (0,)), ((), ())), preferred_element_type=F32)


def segment_positions(segment_ids):
    last_axis = segment_ids.ndim - 1
    index = lax.broadcasted_iota(jnp.int32, segment_ids.shape, last_axis)
    earlier = jnp.concatenate([segment_ids[..., :1] - 1, segment_ids[..., :-1]], axis=-1)
    starts = jnp.where(segment_ids != earlier, index, 0)
    return index - lax.cummax(starts, axis=last_axis)


def rotary_tables(positions):
    half_dim = HD // 2
    steps_float = jnp.arange(half_dim, dtype=F32)
    frequency = jnp.exp(-steps_float * (2.0 * math.log(10000.0) / HD))
    angle = positions.astype(F32)[:, None] * frequency
    cosine, sine = jnp.cos(angle), jnp.sin(angle)
    cos_wide = jnp.concatenate([cosine, cosine], axis=1)
    sin_wide = jnp.concatenate([-sine, sine], axis=1)
    return jnp.concatenate([cos_wide, cos_wide], axis=1), jnp.concatenate([sin_wide, sin_wide], axis=1)


def swap_halves(value):
    heads = [
        pltpu.roll(value[:, h * HD : (h + 1) * HD], HD // 2, 1) for h in range(value.shape[1] // HD)
    ]
    return jnp.concatenate(heads, axis=1)


def normalize(value):
    center = value - jnp.mean(value, axis=-1, keepdims=True)
    inverse = lax.rsqrt(jnp.mean(center * center, axis=-1, keepdims=True) + 1e-05)
    return center * inverse, inverse


def norm_backward(grad_out, normed, inverse, gain):
    scaled = grad_out * gain
    first_mean = jnp.mean(scaled, axis=-1, keepdims=True)
    second_mean = jnp.mean(scaled * normed, axis=-1, keepdims=True)
    return inverse * (scaled - first_mean - normed * second_mean)


def add_norm_sums(sums, grad_out, normed):
    rows, width = grad_out.shape
    sums[0:8, :] += jnp.sum((grad_out * normed).reshape(rows // 8, 8, width), axis=0)
    sums[8:16, :] += jnp.sum(grad_out.reshape(rows // 8, 8, width), axis=0)


def each_rows(rows, action):
    def step(i, carry):
        action(pl.ds(pl.multiple_of(i * STRIP, STRIP), STRIP))
        return carry

    lax.fori_loop(0, rows // STRIP, step, 0, unroll=4)


def received(inner, total, sent, rows):
    return jnp.where(inner[0] == 1, total[rows, :], sent[rows, :]).astype(F32)


def axis_sum(value, axes):
    for axis in axes:
        size, step = lax.axis_size(axis), 1
        while step < size:
            value = value + lax.ppermute(value, axis, [(i, i ^ step) for i in range(size)])
            step *= 2
    return value


def after(value, *others):
    return lax.optimization_barrier((value, *others))[0]


PAIRS = [(0, 1), (1, 0), (2, 3), (3, 2)]
MIDDLE = [(1, 2), (2, 1)]
CYCLE = 4


def run_slots(parts, computes, inner, before, behind):
    count = len(parts)
    held, totals = list(parts), [None] * count
    paired = middle = None
    done = [parts[-1]]
    for slot in range(count + CYCLE * len(computes) - 1):
        roles = {}
        for k in range(count):
            stage, phase = divmod(slot - k, CYCLE)
            if 0 <= stage < len(computes):
                roles[phase] = (k, stage)
        paired = None if paired is None else after(paired, *done)
        middle = None if middle is None else after(middle, *done)
        started, outgoing, arrived = [], [], paired
        if 2 in roles:
            k = roles[2][0]
            outgoing.append(held[k] + middle)
        if 0 in roles:
            outgoing.append(held[roles[0][0]])
        sending = None
        if outgoing:
            sending = outgoing[0] if len(outgoing) == 1 else jnp.where(inner, *outgoing)
            if paired is not None and len(outgoing) == 1:
                sending = after(sending, paired)
            started.append(sending)
        crossing = None
        if 1 in roles:
            k = roles[1][0]
            crossing = held[k] = held[k] + paired
            started.append(crossing)
        if 2 in roles:
            totals[roles[2][0]] = sending
        middle = None if crossing is None else lax.ppermute(crossing, "mp", MIDDLE)
        paired = None if sending is None else lax.ppermute(sending, "mp", PAIRS)
        done = []
        if slot in before:
            started.append(before[slot](*started, arrived))
        if 3 in roles:
            k, stage = roles[3]
            held[k] = computes[stage](k, totals[k], after(arrived, *started))
            done.append(held[k])
        if slot in behind:
            done.append(behind[slot](*done, *started))
        if not done:
            done = started
        if slot + 2 < count:
            done = [*done, parts[slot + 2]]


class Panel:
    def __init__(self, blocks, order, row_blocks):
        count, block, _ = blocks.shape
        self.order = order
        self.half = block // 2
        self.pieces = blocks.reshape(2 * count, self.half, block)
        self.col_blocks = count // row_blocks
        self.count = 2 * row_blocks

    def piece(self, order, place, col_block):
        return (place // 2 * self.col_blocks + col_block) * 2 + place % 2

    def specs(self, width, col_block, col_part):
        out = []
        for place in range(self.count):

            def index(step, order, place=place):
                return (self.piece(order, place, col_block(step)), 0, col_part(step))

            out.append(pl.BlockSpec((None, self.half, width), index))
        return out


class HiddenPanel:
    def __init__(self, slices, order, row_blocks):
        self.slices = slices
        self.order = order
        self.ranks = slices.shape[0] // 2
        self.rows, self.block = slices.shape[2:]
        self.half = self.ranks * self.rows
        self.col_blocks = slices.shape[1] // row_blocks
        self.count = 2 * row_blocks

    def copy(self, copies, slices, place, col_block, target):
        source = slices.at[pl.ds(place % 2 * self.ranks, self.ranks), place // 2 * self.col_blocks + col_block]
        return copies.start(source, target.at[pl.ds(place * self.ranks, self.ranks)])

    def held(self, number):
        return pltpu.VMEM((number, self.count * self.ranks, self.rows, self.block), BF16)


def whole(shape):
    zeros = (0,) * len(shape)
    return pl.BlockSpec(shape, lambda step, *_: zeros)


def params():
    return pltpu.CompilerParams(vmem_limit_bytes=VMEM_LIMIT)


def cost(micros):
    return pl.CostEstimate(flops=0, bytes_accessed=int(micros * 3.5e6), transcendentals=0)


def project(rows, pieces):
    half = pieces[0].shape[0]
    total = dot(rows[:, :half], pieces[0][...])
    for k in range(1, len(pieces)):
        total = total + dot(rows[:, k * half : (k + 1) * half], pieces[k][...])
    return total


def qkv_forward(panel, tokens, cosine, sine, local_width):
    length, width = tokens.shape
    count, half, block = panel.count, panel.half, panel.pieces.shape[2]

    def body(order, x, cos, sin, w_qk, w_v, q_out, k_out, v_out, acc):
        step = pl.program_id(0)

        @pl.when(step == 0)
        def _():
            acc[:, : 2 * local_width] = dot(x[...], w_qk[...])
            acc[:, 2 * local_width :] = dot(x[...], w_v[...])

        @pl.when(step > 0)
        def _():
            acc[:, : 2 * local_width] += dot(x[...], w_qk[...])
            acc[:, 2 * local_width :] += dot(x[...], w_v[...])

        @pl.when(step == count - 1)
        def _():
            for i, out in enumerate((q_out, k_out)):
                for h in range(local_width // HD):
                    value = acc[:, i * local_width + h * HD : i * local_width + (h + 1) * HD]
                    turned = pltpu.roll(value, HD // 2, 1)
                    out[:, h * HD : (h + 1) * HD] = (value * cos[:, :HD] + turned * sin[:, :HD]).astype(BF16)
            v_out[...] = acc[:, 2 * local_width :].astype(BF16)

    def weight(col_block, size):
        return pl.BlockSpec(
            (None, half, size), lambda s, order: (panel.piece(order, s, col_block), 0, 0)
        )

    return pl.pallas_call(
        body,
        grid_spec=pltpu.PrefetchScalarGridSpec(
            num_scalar_prefetch=1,
            grid=(count,),
            in_specs=[
                pl.BlockSpec((length, half), lambda s, order: (0, s)),
                whole((length, PAIR)),
                whole((length, PAIR)),
                weight(0, block),
                weight(1, local_width),
            ],
            out_specs=[whole((length, local_width))] * 3,
            scratch_shapes=[pltpu.VMEM((length, 3 * local_width), F32)],
        ),
        out_shape=[jax.ShapeDtypeStruct((length, local_width), BF16)] * 3,
        compiler_params=params(),
        cost_estimate=cost(11),
        name="qkv_forward",
    )(panel.order, tokens, cosine, sine, panel.pieces, panel.pieces)


def attend(panel, chunk, q, k, v, seg_col, seg_row, key_col, col_key):
    length, local_width = q.shape
    pairs = local_width // PAIR
    count, half = panel.count, panel.half
    width = count * half
    scale = HD**-0.5

    def body(order, q_in, k_in, v_in, segc, segr, keyc, colk, *refs):
        wo = refs[:count]
        p_out, c_out, a_out, acc = refs[count:]
        step = pl.program_id(0)

        @pl.when(step == 0)
        def _():
            acc[...] = jnp.zeros_like(acc)

        visible = (segc[...] == segr[...]) & (colk[...] <= keyc[...])
        for h in range(2):
            lanes = slice(h * HD, (h + 1) * HD)
            scores = dot_nt(q_in[:, lanes], k_in[:, lanes]) * scale
            scores = jnp.where(visible, scores, -1000000000.0)
            exponent = jnp.exp(scores - jnp.max(scores, axis=-1, keepdims=True))
            probs = exponent * (1.0 / jnp.sum(exponent, axis=-1, keepdims=True))
            probs = probs.astype(BF16)
            p_out[h] = probs
            c_out[:, lanes] = dot(probs, v_in[:, lanes]).astype(BF16)
        for i in range(count):
            cols = slice(i * half, (i + 1) * half)
            acc[:, cols] += dot_nt(c_out[...], wo[i][...])

        @pl.when(step == pairs - 1)
        def _():
            a_out[...] = acc[...].astype(BF16)

    all_spec = pl.BlockSpec((length, PAIR), lambda s, *_: (0, s))
    column = pl.BlockSpec((CHUNK, 1), lambda s, *_: (chunk, 0))
    return pl.pallas_call(
        body,
        grid_spec=pltpu.PrefetchScalarGridSpec(
            num_scalar_prefetch=1,
            grid=(pairs,),
            in_specs=[
                pl.BlockSpec((CHUNK, PAIR), lambda s, *_: (chunk, s)),
                all_spec,
                all_spec,
                column,
                whole((1, length)),
                column,
                whole((1, length)),
            ]
            + panel.specs(PAIR, lambda s: 1, lambda s: pairs + s),
            out_specs=[
                pl.BlockSpec((2, CHUNK, length), lambda s, *_: (s, 0, 0)),
                pl.BlockSpec((CHUNK, PAIR), lambda s, *_: (0, s)),
                whole((CHUNK, width)),
            ],
            scratch_shapes=[pltpu.VMEM((CHUNK, width), F32)],
        ),
        out_shape=[
            jax.ShapeDtypeStruct((2 * pairs, CHUNK, length), BF16),
            jax.ShapeDtypeStruct((CHUNK, local_width), BF16),
            jax.ShapeDtypeStruct((CHUNK, width), BF16),
        ],
        compiler_params=params(),
        cost_estimate=cost(7),
        name="attend",
    )(panel.order, q, k, v, seg_col, seg_row, key_col, col_key, *[panel.pieces] * count)


def attend_backward(
    panel, chunk, last, inner, state, q, k, v, probs, context, cosine, sine, carried, g1_before
):
    tokens, norm, attn, grad_two, back = state
    length, local_width = q.shape
    width = tokens.shape[1]
    pairs = local_width // PAIR
    count = panel.count
    scale = HD**-0.5
    first = carried is None

    def body(order, flag, x, gains, t1, s1, g2, t3, s3, q_in, k_in, v_in, p_in, c_in, cos, sin, *refs):
        wo = refs[:count]
        refs = refs[count:]
        if not first:
            kg_in, vg_in = refs[:2]
            refs = refs[3:]
        g1_out, low_out, sums, qg_out, kg_out, vg_out, cg, kg = refs
        step = pl.program_id(0)

        @pl.when(step == 0)
        def _():
            sums[...] = jnp.zeros_like(sums)

            def strip(rows):
                resid = deep_alpha * x[rows, :].astype(F32) + received(flag, t1, s1, rows)
                normed, inverse = normalize(resid)
                grad = deep_alpha * g2[rows, :] + received(flag, t3, s3, rows)
                add_norm_sums(sums, grad, normed)
                grad_one = norm_backward(grad, normed, inverse, gains[0:1, :])
                g1_out[rows, :] = grad_one
                low_out[rows, :] = grad_one.astype(BF16)

            each_rows(CHUNK, strip)

        cg[...] = project(low_out[...], wo).astype(BF16)
        for h in range(2):
            lanes = slice(h * HD, (h + 1) * HD)
            cg_rows = cg[:, lanes]
            row_dot = jnp.sum(cg_rows.astype(F32) * c_in[:, lanes].astype(F32), axis=-1, keepdims=True)
            prob_grad = dot_nt(cg_rows, v_in[:, lanes])
            probs_low = p_in[h]
            score_grad = (probs_low.astype(F32) * (prob_grad - row_dot)).astype(BF16)
            raw = dot(score_grad, k_in[:, lanes]) * scale
            own = pl.ds(chunk * CHUNK, CHUNK)
            turned = pltpu.roll(raw, HD // 2, 1)
            qg_out[:, lanes] = (raw * cos[own, lanes] - turned * sin[own, lanes]).astype(BF16)
            key_grad = dot_tn(score_grad, q_in[:, lanes]) * scale
            value_grad = dot_tn(probs_low, cg_rows)
            if not first:
                key_grad = key_grad + kg_in[:, lanes]
                value_grad = value_grad + vg_in[:, lanes]
            vg_out[:, lanes] = value_grad.astype(vg_out.dtype)
            if last:
                kg[:, lanes] = key_grad
            else:
                kg_out[:, lanes] = key_grad
        if last:
            value = kg[...]
            kg_out[...] = (value * cos[...] - swap_halves(value) * sin[...]).astype(BF16)

    head_spec = pl.BlockSpec((length, PAIR), lambda s, *_: (0, s))
    own_head = pl.BlockSpec((CHUNK, PAIR), lambda s, *_: (0, s))
    rows_spec = whole((CHUNK, width))
    kind = BF16 if last else F32
    in_specs = [pl.BlockSpec((CHUNK, width), lambda s, *_: (chunk, 0)), whole((4, width))]
    in_specs += [rows_spec] * 5
    in_specs += [pl.BlockSpec((CHUNK, PAIR), lambda s, *_: (chunk, s)), head_spec, head_spec]
    in_specs += [pl.BlockSpec((2, CHUNK, length), lambda s, *_: (s, 0, 0)), own_head]
    in_specs += [whole((length, PAIR))] * 2
    in_specs += with_scalars(panel.specs(PAIR, lambda s: 1, lambda s: pairs + s))
    operands = [tokens, norm, *attn, grad_two, *back, q, k, v, probs, context, cosine, sine]
    operands += [panel.pieces] * count
    if not first:
        in_specs += [head_spec] * 2 + any_specs(1)
        operands += [*carried, g1_before]
    g1, low_grad, sums, qg, kg, vg = pl.pallas_call(
        body,
        grid_spec=pltpu.PrefetchScalarGridSpec(
            num_scalar_prefetch=2,
            grid=(pairs,),
            in_specs=in_specs,
            out_specs=[
                pl.BlockSpec((CHUNK, width), lambda s, *_: (chunk, 0)),
                rows_spec,
                whole((16, width)),
                own_head,
                head_spec,
                head_spec,
            ],
            scratch_shapes=[pltpu.VMEM((CHUNK, PAIR), BF16), pltpu.VMEM((length, PAIR), F32)],
        ),
        out_shape=[
            jax.ShapeDtypeStruct((length, width), F32),
            jax.ShapeDtypeStruct((CHUNK, width), BF16),
            jax.ShapeDtypeStruct((16, width), F32),
            jax.ShapeDtypeStruct((CHUNK, local_width), BF16),
            jax.ShapeDtypeStruct((length, local_width), kind),
            jax.ShapeDtypeStruct((length, local_width), kind),
        ],
        input_output_aliases={} if first else {1 + len(operands): 0},
        compiler_params=params(),
        cost_estimate=cost(12),
        name="attend_backward",
    )(panel.order, inner, *operands)
    return g1, low_grad, sums, qg, (kg, vg)


def input_parts(panel, q_grad, k_grad, v_grad):
    chunks = len(q_grad)
    length, local_width = k_grad.shape
    count, half = panel.count, panel.half

    def body(order, *refs):
        qg, kg, vg = refs[:chunks], refs[chunks], refs[chunks + 1]
        wq, wk, wv, out = refs[chunks + 2 :]
        out[...] = (
            dot_nt(stack(qg), wq[...]) + dot_nt(kg[...], wk[...]) + dot_nt(vg[...], wv[...])
        ).astype(BF16)

    def weight(col_block, col_part):
        return pl.BlockSpec(
            (None, half, local_width), lambda s, order: (panel.piece(order, s, col_block), 0, col_part)
        )

    return pl.pallas_call(
        body,
        grid_spec=pltpu.PrefetchScalarGridSpec(
            num_scalar_prefetch=1,
            grid=(count,),
            in_specs=[whole((CHUNK, local_width))] * chunks
            + [whole((length, local_width))] * 2
            + [weight(0, 0), weight(0, 1), weight(1, 0)],
            out_specs=pl.BlockSpec((length, half), lambda s, *_: (0, s)),
        ),
        out_shape=jax.ShapeDtypeStruct((length, count * half), BF16),
        compiler_params=params(),
        cost_estimate=cost(10),
        name="input_parts",
    )(panel.order, *q_grad, k_grad, v_grad, *[panel.pieces] * 3)


def span_of(place, size):
    return pl.ds(pl.multiple_of(place * size, size), size)


def with_scalars(specs):
    return [
        pl.BlockSpec(s.block_shape, lambda step, order, *_, f=s.index_map: f(step, order)) for s in specs
    ]


def copy_received(copies, inner, total, sent, target):
    sem = copies.sems.at[copies.count]
    copies.count += 1
    pl.when(inner == 1)(lambda: pltpu.make_async_copy(total, target, sem).start())
    pl.when(inner != 1)(lambda: pltpu.make_async_copy(sent, target, sem).start())
    return pltpu.make_async_copy(total, target, sem)


class Copies:
    def __init__(self, sems):
        self.sems = sems
        self.count = 0

    def start(self, source, target):
        copy = pltpu.make_async_copy(source, target, self.sems.at[self.count])
        copy.start()
        self.count += 1
        return copy


def wait_all(copies):
    for copy in copies:
        copy.wait()


def held_rows(held, place, k, cols):
    per = TILE // held.shape[2]
    return held[place, k * per : (k + 1) * per, :, cols].reshape(TILE, cols.stop - cols.start)


def rising(rows, held, place, cols):
    total = None
    for k in range(rows.shape[1] // TILE):
        product = dot(rows[:, k * TILE : (k + 1) * TILE], held_rows(held, place, k, cols))
        total = product if total is None else total + product
    return total


def falling(acc, value, held, place, cols, first):
    for k in range(acc.shape[1] // TILE):
        span = slice(k * TILE, (k + 1) * TILE)
        product = dot_nt(value, held_rows(held, place, k, cols))
        if first:
            acc[:, span] = product
        else:
            acc[:, span] += product


def any_specs(count):
    return [pl.BlockSpec(memory_space=pl.ANY)] * count


def ffn_forward(panel, chunk, scalars, tokens, norm, total, sent, before):
    width = tokens.shape[1]
    block = panel.block
    span = HCAP // block
    own = pl.ds(chunk * CHUNK, CHUNK)

    def body(order, flags, gains, x_in, t_in, s_in, slices, *refs):
        refs = refs[len(before) :]
        hid_out, low_out, act_out, slope_out, inner_out, f_out = refs[:6]
        x, t1, hid, low, act, slope, inner, f, acc, held, sems = refs[6:]
        copies = Copies(sems)
        rows_in = [copy_received(copies, flags[0], t_in, s_in, t1), copies.start(x_in.at[own], x)]
        weights = {
            (tile, group): [
                panel.copy(copies, slices, k, group * span + tile, held.at[tile * 3 + group])
                for k in range(panel.count)
            ]
            for tile in range(span)
            for group in range(3)
        }
        wait_all(rows_in)

        def norm_strip(rows):
            resid = deep_alpha * x[rows, :].astype(F32) + t1[rows, :].astype(F32)
            normed, _ = normalize(resid)
            value = normed * gains[0:1, :] + gains[1:2, :]
            hid[rows, :] = value
            low[rows, :] = value.astype(BF16)

        each_rows(CHUNK, norm_strip)
        out = [copies.start(hid, hid_out), copies.start(low, low_out.at[own])]
        root = math.sqrt(2.0 / math.pi)
        for tile in range(span):
            wait_all(weights[tile, 0])
            wait_all(weights[tile, 1])
            for part in range(block // TILE):
                cols = slice(part * TILE, (part + 1) * TILE)
                gate = rising(low, held, tile * 3, cols)
                up = rising(low, held, tile * 3 + 1, cols)
                lane = lax.broadcasted_iota(jnp.int32, (1, TILE), 1) + (tile * block + part * TILE)
                live = (lane < flags[1]).astype(F32)
                square = gate * gate
                bend = jnp.tanh(root * gate * (1.0 + 0.044715 * square))
                low_half = 0.5 * (1.0 + bend)
                value = gate * low_half * live
                rise = low_half + 0.5 * gate * (1.0 - bend * bend) * (root * (1.0 + 0.134145 * square))
                act[tile, :, cols] = value.astype(BF16)
                slope[tile, :, cols] = (rise * up * live).astype(BF16)
                inner[tile, :, cols] = (value * up).astype(BF16)
                if part == 0:
                    wait_all(weights[tile, 2])
                falling(acc, inner[tile, :, cols], held, tile * 3 + 2, cols, tile == 0 and part == 0)
            cols = pl.ds(tile * block, block)
            for ref, target in ((act, act_out), (slope, slope_out)):
                out.append(copies.start(ref.at[tile], target.at[:, cols]))
            out.append(copies.start(inner.at[tile], inner_out.at[own, cols]))
        f[...] = acc[...].astype(BF16)
        out.append(copies.start(f, f_out))
        wait_all(out)

    tile_shape = jax.ShapeDtypeStruct((CHUNK, HCAP), BF16)
    low_shape = jax.ShapeDtypeStruct((CHUNK, width), BF16)
    low_rows = pltpu.VMEM((CHUNK, width), BF16)
    wide_rows = pltpu.VMEM((CHUNK, width), F32)
    tiles = pltpu.VMEM((span, CHUNK, block), BF16)
    return pl.pallas_call(
        body,
        grid_spec=pltpu.PrefetchScalarGridSpec(
            num_scalar_prefetch=2,
            grid=(1,),
            in_specs=[whole((4, width))] + any_specs(4 + len(before)),
            out_specs=any_specs(6),
            scratch_shapes=[low_rows] * 2
            + [wide_rows, low_rows]
            + [tiles] * 3
            + [low_rows, wide_rows]
            + [
                panel.held(span * 3),
                pltpu.SemaphoreType.DMA((6 + span * (3 * panel.count + 3),)),
            ],
        ),
        out_shape=[
            jax.ShapeDtypeStruct((CHUNK, width), F32),
            jax.ShapeDtypeStruct(tokens.shape, BF16),
            tile_shape,
            tile_shape,
            jax.ShapeDtypeStruct((tokens.shape[0], HCAP), BF16),
            low_shape,
        ],
        input_output_aliases={7: 1, 8: 4} if before else {},
        compiler_params=params(),
        cost_estimate=cost(14),
        name="ffn_forward",
    )(panel.order, scalars, norm, tokens, total, sent, panel.slices, *before)


def ffn_backward(
    panel, chunk, inner, group_weight, hidden, norm, total, sent, out_grad, act, slope, before
):
    width = hidden.shape[1]
    block = panel.block
    span = HCAP // block
    own = pl.ds(chunk * CHUNK, CHUNK)

    def body(order, flags, scale, gains, hid_in, t_in, s_in, og_in, act_in, slope_in, slices, *refs):
        refs = refs[len(before) :]
        y_out, g2_out, low_out, sums, gate_out, up_out, h_out = refs[:7]
        hid, t2, og, act_rows, slope_rows, y, g2, low, gate, up, h, acc, held, sems = refs[7:]
        copies = Copies(sems)
        rows_in = [copies.start(hid_in, hid), copies.start(og_in.at[own], og)]
        rows_in.append(copy_received(copies, flags[0], t_in, s_in, t2))
        saved = [copies.start(act_in, act_rows), copies.start(slope_in, slope_rows)]
        weights = {
            (tile, group): [
                panel.copy(copies, slices, k, group * span + tile, held.at[tile * 3 + group])
                for k in range(panel.count)
            ]
            for tile in range(span)
            for group in (2, 0, 1)
        }
        sums[...] = jnp.zeros_like(sums)
        wait_all(rows_in)

        def norm_strip(rows):
            resid = deep_alpha * hid[rows, :] + t2[rows, :].astype(F32)
            normed, inverse = normalize(resid)
            y[rows, :] = (normed * gains[2:3, :] + gains[3:4, :]).astype(BF16)
            grad = scale[0] * og[rows, :].astype(F32)
            add_norm_sums(sums, grad, normed)
            grad_two = norm_backward(grad, normed, inverse, gains[2:3, :])
            g2[rows, :] = grad_two
            low[rows, :] = grad_two.astype(BF16)

        each_rows(CHUNK, norm_strip)
        out = [copies.start(a, b) for a, b in ((y, y_out.at[own]), (g2, g2_out), (low, low_out.at[own]))]
        wait_all(saved)
        for tile in range(span):
            wait_all(weights[tile, 2])
            for part in range(block // TILE):
                cols = slice(part * TILE, (part + 1) * TILE)
                saved_cols = slice(tile * block + part * TILE, tile * block + (part + 1) * TILE)
                inner_grad = rising(low, held, tile * 3 + 2, cols)
                gate_grad = (inner_grad * slope_rows[:, saved_cols].astype(F32)).astype(BF16)
                up_grad = (inner_grad * act_rows[:, saved_cols].astype(F32)).astype(BF16)
                gate[tile, :, cols] = gate_grad
                up[tile, :, cols] = up_grad
                if part == 0:
                    wait_all(weights[tile, 0])
                    wait_all(weights[tile, 1])
                falling(acc, gate_grad, held, tile * 3, cols, tile == 0 and part == 0)
                falling(acc, up_grad, held, tile * 3 + 1, cols, False)
            cols = pl.ds(tile * block, block)
            for ref, target in ((gate, gate_out), (up, up_out)):
                out.append(copies.start(ref.at[tile], target.at[own, cols]))
        h[...] = acc[...].astype(BF16)
        out.append(copies.start(h, h_out))
        wait_all(out)

    operands = [norm, hidden, total, sent, out_grad, act, slope, panel.slices]
    operands += before
    wide_tile_shape = jax.ShapeDtypeStruct((out_grad.shape[0], HCAP), BF16)
    low_shape = jax.ShapeDtypeStruct((CHUNK, width), BF16)
    low_rows = pltpu.VMEM((CHUNK, width), BF16)
    wide_rows = pltpu.VMEM((CHUNK, width), F32)
    tiles = pltpu.VMEM((span, CHUNK, block), BF16)
    return pl.pallas_call(
        body,
        grid_spec=pltpu.PrefetchScalarGridSpec(
            num_scalar_prefetch=3,
            grid=(1,),
            in_specs=[whole((4, width))] + any_specs(len(operands) - 1),
            out_specs=any_specs(3) + [whole((16, width))] + any_specs(3),
            scratch_shapes=[wide_rows, low_rows, low_rows]
            + [pltpu.VMEM((CHUNK, HCAP), BF16)] * 2
            + [low_rows, wide_rows, low_rows, tiles, tiles, low_rows, wide_rows]
            + [
                panel.held(span * 3),
                pltpu.SemaphoreType.DMA((10 + span * (3 * panel.count + 2),)),
            ],
        ),
        out_shape=[
            jax.ShapeDtypeStruct(out_grad.shape, BF16),
            jax.ShapeDtypeStruct((CHUNK, width), F32),
            jax.ShapeDtypeStruct(out_grad.shape, BF16),
            jax.ShapeDtypeStruct((16, width), F32),
            wide_tile_shape,
            wide_tile_shape,
            low_shape,
        ],
        input_output_aliases={11 + i: out for i, out in enumerate((0, 2, 4, 5)[: len(before)])},
        compiler_params=params(),
        cost_estimate=cost(20),
        name="ffn_backward",
    )(panel.order, inner, group_weight, *operands)


def stack(refs):
    return jnp.concatenate([r[...] for r in refs], axis=0)


def turn(left, refs):
    left[...] = stack(refs).T


def grad_outputs(block, blocks, ranks, full=False):
    half = block // 2
    if full:
        return (
            pl.BlockSpec((2 * ranks, None, half // ranks, block), lambda s, *_: (0, s, 0, 0)),
            jax.ShapeDtypeStruct((2 * ranks, blocks, half // ranks, block), BF16),
        )
    if ranks is None:
        return (
            pl.BlockSpec((None, half, block), lambda s, *_: (s, 0, 0)),
            jax.ShapeDtypeStruct((blocks, half, block), BF16),
        )
    return (
        pl.BlockSpec((ranks, None, half // ranks, block), lambda s, *_: (0, s, 0, 0)),
        jax.ShapeDtypeStruct((ranks, blocks, half // ranks, block), BF16),
    )


def ffn_weight_grads(which, left, rights, ranks=None, arrived=None, full=False):
    length, width = left.shape
    block = width // 2
    half = block // 2
    span = HCAP // block
    per_row = len(rights) * span

    rows = block if full else half

    def body(core, g, *refs):
        out, turned = refs[-2:]
        step = pl.program_id(0) % per_row

        @pl.when(step == 0)
        def _():
            turned[...] = g[...].T

        def write(right):
            result = dot(turned[...], right[...])
            if arrived is not None:
                result = result + refs[len(rights)][...].astype(F32)
            out[...] = result.astype(BF16).reshape(out.shape)

        for i, right in enumerate(refs[: len(rights)]):
            pl.when(step // span == i)(lambda right=right: write(right))

    def right_spec(group):
        return pl.BlockSpec(
            (length, block), lambda s, core: (0, jnp.clip(s % per_row - group * span, 0, span - 1))
        )

    if full:
        left_spec = pl.BlockSpec((length, rows), lambda s, core: (0, s // per_row))
    else:
        left_spec = pl.BlockSpec((length, rows), lambda s, core: (0, s // per_row * 2 + core[0]))
    in_specs = [left_spec] + [right_spec(i) for i in range(len(rights))]
    operands = [left, *rights]
    blocks = width // block * per_row
    if arrived is not None:
        in_specs.append(pl.BlockSpec((None, half, block), lambda s, core: (s, 0, 0)))
        operands.append(arrived)
    out_spec, out_shape = grad_outputs(block, blocks, ranks, full)
    return pl.pallas_call(
        body,
        grid_spec=pltpu.PrefetchScalarGridSpec(
            num_scalar_prefetch=1,
            grid=(blocks,),
            in_specs=in_specs,
            out_specs=out_spec,
            scratch_shapes=[pltpu.VMEM((rows, length), BF16)],
        ),
        out_shape=out_shape,
        compiler_params=params(),
        cost_estimate=cost(15),
        name="ffn_weight_grads",
    )(which, *operands)


def halving_bits(ranks, row_block):
    bits = [1 << i for i in range(ranks.bit_length() - 1)]
    return bits if row_block % 2 == 0 else bits[::-1]


def halving_keys(ranks, row_block):
    bits = halving_bits(ranks, row_block)
    return [
        sum(bit for j, bit in enumerate(bits) if i >> (len(bits) - 1 - j) & 1) for i in range(ranks)
    ]


def attention_weight_grads(which, tokens, q_grad, k_grad, v_grad, attn_grad, context, ranks=None, arrived=None):
    length, width = tokens.shape
    chunks = len(context)
    local_width = k_grad.shape[1]
    block = 2 * local_width
    half = block // 2
    row_blocks = width // block
    outputs = 1 if ranks is None else 2 * row_blocks
    rows = half // (ranks or 1)

    def body(core, x, kg, vg, *refs):
        qg, ctx, g = (refs[i * chunks : (i + 1) * chunks] for i in range(3))
        refs = refs[3 * chunks :]
        outs, turned, held = refs[-2 - outputs : -2], refs[-2], refs[-1]
        row_block, step = pl.program_id(0) // 2, pl.program_id(0) % 2

        def write(start, right):
            cols = slice(start, start + local_width)
            result = dot(turned[...], right)
            if arrived is not None:
                result = result + refs[0][:, cols].astype(F32)
            result = result.astype(BF16)
            if ranks is None:
                outs[0][:, cols] = result
                return
            held[...] = result
            for r in range(row_blocks):

                @pl.when(row_block == r)
                def _(r=r):
                    for i, key in enumerate(halving_keys(ranks, r)):
                        own = span_of(core[1] ^ key, rows)
                        outs[2 * r + i // (ranks // 2)][i % (ranks // 2), :, cols] = held[own, :]

        @pl.when(step == 0)
        def _():
            turned[...] = x[...].T
            write(0, stack(qg))
            write(local_width, kg[...])

        @pl.when(step == 1)
        def _():
            write(0, vg[...])
            turn(turned, g)
            write(local_width, stack(ctx))

    in_specs = [pl.BlockSpec((length, half), lambda s, core: (0, s // 2 * 2 + core[0]))]
    in_specs += [whole((length, local_width))] * 2
    in_specs += [whole((CHUNK, local_width))] * (2 * chunks)
    in_specs += [pl.BlockSpec((CHUNK, half), lambda s, core: (0, s // 2 * 2 + core[0]))] * chunks
    operands = [tokens, k_grad, v_grad, *q_grad, *context, *attn_grad]
    if arrived is not None:
        in_specs.append(pl.BlockSpec((None, half, block), lambda s, core: (s, 0, 0)))
        operands.append(arrived)
    if ranks is None:
        out_specs = [pl.BlockSpec((None, half, block), lambda s, *_: (s, 0, 0))]
        out_shape = [jax.ShapeDtypeStruct((2 * row_blocks, half, block), BF16)]
    else:
        out_specs = [
            pl.BlockSpec(
                (ranks // 2, None, rows, block), lambda s, *_, r=i // 2: (0, jnp.clip(s - 2 * r, 0, 1), 0, 0)
            )
            for i in range(outputs)
        ]
        out_shape = [jax.ShapeDtypeStruct((ranks // 2, 2, rows, block), BF16)] * outputs
    return pl.pallas_call(
        body,
        grid_spec=pltpu.PrefetchScalarGridSpec(
            num_scalar_prefetch=1,
            grid=(2 * row_blocks,),
            in_specs=in_specs,
            out_specs=out_specs,
            scratch_shapes=[pltpu.VMEM((half, length), BF16), pltpu.VMEM((half, local_width), BF16)],
        ),
        out_shape=out_shape,
        compiler_params=params(),
        cost_estimate=cost(9),
        name="attention_weight_grads",
    )(which, *operands)


SWAP = [(0, 1), (1, 0)]


class Group:
    def __init__(self, grads):
        self.grads = grads
        self.core = lax.axis_index("obj").astype(jnp.int32).reshape(1)

    def make_away(self, *others):
        self.away = self.grads(after(1 - self.core, *others), None, None)
        return self.away

    def send(self, *others):
        self.arrived = lax.ppermute(after(self.away, *others), "obj", SWAP)
        return self.away

    def reduce(self, earlier, *others):
        own = self.grads(self.core, lax.axis_size("dp"), after(self.arrived, *others))
        operand = after(own, *[group.sum for group in earlier])
        self.sum = lax.psum_scatter(operand, "dp", scatter_dimension=0, tiled=True)[0]
        return own

    def reduce_whole(self, *others):
        own = self.grads(after(self.core, *others), lax.axis_size("dp"), None, True)
        self.sum = lax.psum_scatter(own, ("obj", "dp"), scatter_dimension=0, tiled=True)[0]
        return own


def pick_slices(places, groups, sizes):
    rows, block = groups[0].shape[1:]
    ends, total = [], 0
    for group in groups:
        total += group.shape[0]
        ends.append(total)
    targets = [(array, place) for array, size in enumerate(sizes) for place in range(size)]

    def body(place, *refs):
        sources, outs = refs[: len(groups)], refs[len(groups) : -3]
        held, into, out_of = refs[-3:]
        for i in range(len(targets)):
            for g, source in enumerate(sources):
                first = ends[g - 1] if g else 0

                @pl.when((place[i] >= first) & (place[i] < ends[g]))
                def _(source=source, first=first, i=i):
                    pltpu.make_async_copy(source.at[place[i] - first], held.at[i], into.at[i]).start()

        copies = []
        for i, (array, spot) in enumerate(targets):
            pltpu.make_async_copy(sources[0].at[0], held.at[i], into.at[i]).wait()
            copy = pltpu.make_async_copy(held.at[i], outs[array].at[spot], out_of.at[i])
            copy.start()
            copies.append(copy)
        wait_all(copies)

    return pl.pallas_call(
        body,
        grid_spec=pltpu.PrefetchScalarGridSpec(
            num_scalar_prefetch=1,
            grid=(1,),
            in_specs=any_specs(len(groups)),
            out_specs=any_specs(len(sizes)),
            scratch_shapes=[pltpu.VMEM((len(targets), rows, block), BF16)]
            + [pltpu.SemaphoreType.DMA((len(targets),))] * 2,
        ),
        out_shape=[jax.ShapeDtypeStruct((size, rows, block), BF16) for size in sizes],
        compiler_params=params(),
        cost_estimate=cost(5),
        name="pick_slices",
    )(places, *groups)


def place_blocks(starts, sources):
    slices, count, rows, block = sources[0].shape
    total = len(sources) * slices

    def body(begin, *refs):
        parts, out, held, into, out_of = refs[:-4], *refs[-4:]
        arriving, leaving = [], []
        for i in range(total):
            copy = pltpu.make_async_copy(parts[i // slices].at[i % slices], held.at[i], into.at[i])
            copy.start()
            arriving.append(copy)
        for i in range(total):
            arriving[i].wait()
            own = pl.ds(pl.multiple_of(begin[i], rows), rows)
            for j in range(count):
                target = out.at[i // slices // 2 * count + j, own]
                copy = pltpu.make_async_copy(held.at[i, j], target, out_of.at[i * count + j])
                copy.start()
                leaving.append(copy)
        wait_all(leaving)

    return pl.pallas_call(
        body,
        grid_spec=pltpu.PrefetchScalarGridSpec(
            num_scalar_prefetch=1,
            grid=(1,),
            in_specs=any_specs(len(sources)),
            out_specs=pl.BlockSpec(memory_space=pl.ANY),
            scratch_shapes=[
                pltpu.VMEM((total, count, rows, block), BF16),
                pltpu.SemaphoreType.DMA((total,)),
                pltpu.SemaphoreType.DMA((total * count,)),
            ],
        ),
        out_shape=jax.ShapeDtypeStruct((len(sources) // 2 * count, block, block), BF16),
        compiler_params=params(),
        cost_estimate=cost(6),
        name="place_blocks",
    )(starts, *sources)


def gather_block(starts, slices, grad):
    for i, piece in enumerate(slices):
        rows = piece.shape[0]
        grad[pl.ds(pl.multiple_of(starts[i], rows), rows), :] = piece[...]


def update_blocks(first, starts, scales, slices, roots_left, roots_right, weights, stats_left, stats_right, before):
    count, piece_rows, block = slices[0].shape
    half = block // 2
    steps = 4

    def body(begin, factor, *refs):
        pieces, refs = refs[: len(slices)], refs[len(slices) :]
        left, right, w, sl, sr = refs[:5]
        c_out, w_out, l_out, r_out, grad, inner, shaped, trust = refs[5 + len(before) :]
        slot, part = pl.program_id(0) + first, pl.program_id(1)
        clip = factor[0, slot]

        @pl.when(part == 0)
        def _():
            gather_block(begin, pieces, grad)
            low = (grad[...].astype(F32) * clip).astype(BF16)
            inner[...] = dot(left[...], low).astype(BF16)

        @pl.when(part == 1)
        def _():
            value = dot(inner[...], right[...])
            shaped[...] = value
            energy = jnp.sum(value * value) * (1.0 / (block * block))
            trust[...] = factor[2, slot] / jnp.sqrt(jnp.full((8, 128), energy, F32) + 1e-06)

        @pl.when(part >= 2)
        def _():
            rows = pl.ds(pl.multiple_of((part - 2) * half, half), half)
            w_out[...] = w[...] - trust[0:1, 0:1] * shaped[rows, :]
            own = grad[rows, :]
            c_out[...] = own.astype(F32) * clip
            square = factor[1, slot]
            l_out[...] = stat_decay * sl[...] + square * dot_nt(own, grad[...])
            r_out[...] = stat_decay * sr[...] + square * dot_tn(grad[:, rows], grad[...])

    def ahead(from_step):
        return lambda s, p, *_: jnp.minimum(s + (p >= from_step).astype(jnp.int32), count - 1)

    def full(place):
        return pl.BlockSpec((None, block, block), lambda s, p, *_: (first + place(s, p), 0, 0))

    piece = pl.BlockSpec((None, piece_rows, block), lambda s, p, *_: (ahead(3)(s, p), 0, 0))
    right_place = lambda s, p: jnp.maximum(s - (p < 1).astype(jnp.int32), 0)
    half_spec = pl.BlockSpec((None, half, block), lambda s, p, *_: (first + s, jnp.maximum(p - 2, 0), 0))
    out = jax.ShapeDtypeStruct(weights.shape, F32)
    in_specs = [piece] * len(slices) + [full(ahead(3)), full(right_place)] + [half_spec] * 3
    return pl.pallas_call(
        body,
        grid_spec=pltpu.PrefetchScalarGridSpec(
            num_scalar_prefetch=2,
            grid=(count, steps),
            in_specs=in_specs + any_specs(len(before)),
            out_specs=[half_spec] * 4,
            scratch_shapes=[
                pltpu.VMEM((block, block), BF16),
                pltpu.VMEM((block, block), BF16),
                pltpu.VMEM((block, block), F32),
                pltpu.VMEM((8, 128), F32),
            ],
        ),
        out_shape=[out] * 4,
        input_output_aliases={2 + len(in_specs) + i: i for i in range(len(before))},
        compiler_params=params(),
        cost_estimate=cost(14 * count),
        name="update_blocks",
    )(starts, scales, *slices, roots_left, roots_right, weights, stats_left, stats_right, *before)


def norm_sums(sums):
    return jnp.sum(sum(sums).reshape(2, 8, -1), axis=1)


def per_device(
    layer_input,
    out_grad,
    segment_ids,
    target_flags,
    hidden_units,
    block_slot,
    weight_blocks,
    stats_left,
    stats_right,
    roots_left,
    roots_right,
    norm_params,
    norm_moments,
):
    row_count, length, width = layer_input.shape
    local_width = HEADS // lax.axis_size("mp") * HD
    owned_slots, block = weight_blocks.shape[1], weight_blocks.shape[-1]
    half = block // 2
    slots = block_slot.shape[1]
    core = lax.axis_index("obj")

    master = weight_blocks[0]
    ranks, rank = lax.axis_size("dp"), lax.axis_index("dp").astype(jnp.int32)
    rows, row_blocks = half // ranks, width // block
    core_row = core.astype(jnp.int32) * half
    received_slices = [None] * ranks
    for k in [*range(1, ranks), 0]:
        first_row = core_row + (rank ^ k) * rows
        piece = lax.dynamic_slice(master, (0, first_row, 0), (owned_slots, rows, block)).astype(BF16)
        received_slices[k] = lax.ppermute(piece, "dp", [(i, i ^ k) for i in range(ranks)]) if k else piece
    by_place = block_slot[0].reshape(row_blocks, -1)
    attention_blocks = 4 * local_width // block
    panel_slots = jnp.concatenate([by_place[:, :attention_blocks].reshape(-1), by_place[:, attention_blocks:].reshape(-1)])
    weight_energy = jnp.mean(master * master, axis=(1, 2))
    low_left, low_right = roots_left[0].astype(BF16), roots_right[0].astype(BF16)
    sources = ((panel_slots // owned_slots) ^ rank) * owned_slots + panel_slots % owned_slots
    sources, weight_energy, low_left, low_right = lax.optimization_barrier(
        (sources, weight_energy, low_left, low_right)
    )
    sizes = [attention_blocks] * row_blocks + [slots - attention_blocks * row_blocks]
    *attention_slices, hidden_slices = pick_slices(sources, received_slices, sizes)
    hidden_panel = HiddenPanel(
        lax.all_gather(hidden_slices, ("obj", "dp"), axis=0), block_slot[0], row_blocks
    )
    parts_held, part_starts = [], []
    for row_block, held in enumerate(attention_slices):
        held, keys = held[None], [0]
        bits = [1 << i for i in range(ranks.bit_length() - 1)]
        for bit in bits if row_block % 2 == 0 else bits[::-1]:
            arriving = lax.ppermute(held, "dp", [(i, i ^ bit) for i in range(ranks)])
            held = jnp.concatenate([held, arriving])
            keys = keys + [key ^ bit for key in keys]
        parts_held += [held, lax.ppermute(held, "obj", SWAP)]
        first_rows = (rank ^ jnp.array(keys, jnp.int32)) * rows
        part_starts += [core_row + first_rows, half - core_row + first_rows]
    panel = Panel(place_blocks(jnp.concatenate(part_starts), parts_held), block_slot[0], row_blocks)

    flags = target_flags.reshape(length)
    own_count = jnp.sum(flags.astype(F32))
    total_count = axis_sum(own_count, ("obj", "dp"))
    group_total = lax.axis_size("obj") * lax.axis_size("dp")
    group_weight = own_count * group_total / total_count

    segments = segment_ids.reshape(length)
    cosine, sine = rotary_tables(segment_positions(segment_ids)[0])
    cosine, group_weight = lax.optimization_barrier((cosine, group_weight))
    index = jnp.arange(length, dtype=jnp.int32)
    in_span = (flags == 1) & (core == 1)
    key_col = jnp.where(in_span, index, -1)[:, None]
    col_key = jnp.where(in_span, index, -1)[None, :]

    tokens = layer_input.reshape(length, width)
    chunks = range(length // CHUNK)
    parts = [slice(c * CHUNK, (c + 1) * CHUNK) for c in chunks]
    query, keys_rot, values = qkv_forward(panel, tokens, cosine, sine, local_width)
    masks = (segments[:, None], segments[None, :], key_col, col_key)
    attended = [attend(panel, c, query, keys_rot, values, *masks) for c in chunks]
    probs, context, attn_part = zip(*attended)
    place = lax.axis_index("mp")
    inner_flag = ((place == 1) | (place == 2)).astype(jnp.int32).reshape(1)
    scalars = jnp.concatenate([inner_flag, hidden_units])
    weight_scalar = group_weight.reshape(1)
    flat_out_grad = out_grad.reshape(length, width)
    attn, ahead, back, turned = {}, {}, {}, {}

    def ffn_ahead(c, total, sent):
        attn[c] = (total, sent)
        before = [ahead[c - 1][i] for i in (1, 4)] if c else []
        ahead[c] = ffn_forward(hidden_panel, c, scalars, tokens, norm_params, total, sent, before)
        return ahead[c][5]

    def ffn_back(c, total, sent):
        hidden, _, act, slope, _, _ = ahead[c]
        saved = (hidden, norm_params, total, sent, flat_out_grad, act, slope)
        before = [back[c - 1][i] for i in (0, 2, 4, 5)] if c else []
        back[c] = ffn_backward(hidden_panel, c, inner_flag, weight_scalar, *saved, before)
        return back[c][6]

    def attention_back(c, total, sent):
        if c == len(chunks) - 1:
            total = after(total, down.sum)
        state = (tokens, norm_params, attn[c], back[c][1], (total, sent))
        heads = (query, keys_rot, values, probs[c], context[c], cosine, sine)
        carried = turned[c - 1][4] if c else None
        g1_before = turned[c - 1][0] if c else None
        last = c == len(chunks) - 1
        turned[c] = attend_backward(panel, c, last, inner_flag, state, *heads, carried, g1_before)
        return turned[c][2]

    def each_of(results, i):
        return [results[c][i] for c in chunks]

    last_chunk = chunks[-1]

    def down_grads(which, *opts):
        return ffn_weight_grads(which, back[last_chunk][2], [ahead[last_chunk][4]], *opts)

    def gate_up_grads(which, *opts):
        return ffn_weight_grads(which, ahead[last_chunk][1], list(back[last_chunk][4:6]), *opts)

    def attention_grads(which, *opts):
        heads = (each_of(turned, 3), *turned[chunks[-1]][4], each_of(turned, 1), context)
        return attention_weight_grads(which, tokens, *heads, *opts)

    down, gate_up = Group(down_grads), Group(gate_up_grads)

    first = len(chunks) - 1 + 2 * CYCLE
    before = {
        first: down.reduce_whole,
        first + 1: gate_up.send,
        first + 2: lambda *others: gate_up.reduce((), *others),
    }
    behind = {first: gate_up.make_away}
    run_slots(attn_part, (ffn_ahead, ffn_back, attention_back), inner_flag[0] == 1, before, behind)
    y_out = back[chunks[-1]][0].reshape(row_count, length, width)
    sums_two = each_of(back, 3)
    sums_one, query_grad = each_of(turned, 2), each_of(turned, 3)
    def squares(value):
        wide = value.astype(F32)
        return jnp.sum(wide * wide)

    own_core = core.astype(jnp.int32)
    (away,) = attention_grads(jnp.stack([1 - own_core, rank]))
    arrived = lax.ppermute(away, "obj", SWAP)
    input_part = input_parts(panel, [after(query_grad[0], away)] + query_grad[1:], *turned[chunks[-1]][4])
    own_norm_grad = jnp.concatenate([norm_sums(sums_one), norm_sums(sums_two)])
    norm_grad = axis_sum(after(own_norm_grad, away), ("obj", "dp"))
    halved = attention_grads(jnp.stack([own_core, rank]), ranks, after(arrived, input_part, norm_grad))
    early_squares = squares(gate_up.sum) + squares(down.sum)
    attention_sums = []
    for row_block in range(row_blocks):
        kept, sent = halved[2 * row_block : 2 * row_block + 2]
        for bit in halving_bits(ranks, row_block):
            arriving = lax.ppermute(sent, "dp", [(i, i ^ bit) for i in range(ranks)])
            if kept.shape[0] == 1:
                arriving = after(arriving, early_squares)
            total = kept + arriving
            kept, sent = total[: total.shape[0] // 2], total[total.shape[0] // 2 :]
        attention_sums.append(total[0])
    input_sum = lax.psum(after(input_part, gate_up.sum), "mp")

    groups = (*attention_sums, gate_up.sum, down.sum)
    own_squares = axis_sum(early_squares + sum(squares(group) for group in attention_sums), ("mp",))
    others = rank ^ jnp.arange(ranks, dtype=jnp.int32)
    col_blocks = slots // (width // block)
    place_of, firsts, base = [0] * slots, (0, 2, 2 + 2 * (HCAP // block), col_blocks), 0
    for first, stop in zip(firsts, firsts[1:]):
        for row_block in range(width // block):
            for col_block in range(first, stop):
                place_of[row_block * col_blocks + col_block] = base
                base += 1
    slot_index = jnp.arange(slots, dtype=jnp.int32)
    at_slot = jnp.sum(
        jnp.where(block_slot[0][None, :] == slot_index[:, None], jnp.array(place_of, jnp.int32)[None, :], 0),
        axis=1,
    )
    wanted = jnp.take(at_slot.reshape(ranks, owned_slots), others, axis=0).reshape(-1)
    halves = 2 if owned_slots % 2 == 0 else 1
    each = owned_slots // halves
    wanted = wanted.reshape(ranks, halves, each).transpose(1, 0, 2).reshape(-1)
    picked = pick_slices(wanted, groups, [each] * (halves * ranks))
    first_rows = others * rows
    starts = jnp.concatenate([core_row + first_rows, half - core_row + first_rows])
    low_roots = (low_left, low_right)

    def exchange(part, *earlier):
        pieces = [after(piece, *earlier) for piece in picked[part * ranks : (part + 1) * ranks]]
        mine = [
            lax.ppermute(piece, "dp", [(i, i ^ k) for i in range(ranks)]) if k else piece
            for k, piece in enumerate(pieces)
        ]
        return mine

    def hand_over(mine):
        return mine + [lax.ppermute(piece, "obj", SWAP) for piece in mine]

    rank_squares = [own_squares] + [
        lax.ppermute(own_squares, "dp", [(i, i ^ k) for i in range(ranks)]) for k in range(1, ranks)
    ]
    core_squares = jnp.sum(jnp.stack(rank_squares)[others])
    block_squares = axis_sum(core_squares, ("obj",))
    grad_norm = jnp.sqrt(block_squares + jnp.sum(norm_grad * norm_grad))
    clip_factor = 1.0 / jnp.maximum(grad_norm, 1.0)

    exchanged = [exchange(0, *rank_squares)]
    if halves == 2:
        exchanged.append(exchange(1, *exchanged[0], clip_factor))
    clips = jnp.full((owned_slots,), clip_factor, F32)
    scales = jnp.stack([clips, (1.0 - stat_decay) * clips * clips, block_rate * jnp.sqrt(weight_energy)])
    results = ()
    for part in range(halves):
        slices = hand_over([after(piece, *results[:1]) for piece in exchanged[part]])
        results = update_blocks(
            part * each, starts, scales, slices, *low_roots, master, stats_left[0], stats_right[0], results
        )
    clipped, new_weights, new_left, new_right = results
    x_grad = (deep_alpha * turned[chunks[-1]][0] + input_sum.astype(F32)).astype(BF16)
    x_grad = x_grad.reshape(row_count, length, width)
    param_clipped = norm_grad * clip_factor
    new_moments = 0.5 * norm_moments + 0.5 * param_clipped * param_clipped
    new_params = norm_params - param_rate * param_clipped / (jnp.sqrt(new_moments) + 1e-08)
    return (
        y_out,
        x_grad,
        clipped[None],
        new_weights[None],
        new_left[None],
        new_right[None],
        param_clipped,
        new_moments,
        new_params,
        grad_norm,
    )


def solution(mesh):
    return jax.shard_map(
        per_device,
        mesh=mesh,
        in_specs=(
            P(("obj", "dp"), None, None),
            P(("obj", "dp"), None, None),
            P(("obj", "dp"), None),
            P(("obj", "dp"), None),
            P("mp"),
            P("mp", None),
            P("mp", "dp", None, None),
            P("mp", "dp", None, None),
            P("mp", "dp", None, None),
            P("mp", "dp", None, None),
            P("mp", "dp", None, None),
            P(),
            P(),
        ),
        out_specs=(
            P(("obj", "dp"), None, None),
            P(("obj", "dp"), None, None),
            P("mp", "dp", None, None),
            P("mp", "dp", None, None),
            P("mp", "dp", None, None),
            P("mp", "dp", None, None),
            P(),
            P(),
            P(),
            P(),
        ),
        check_vma=False,
    )
```
